256 devices in a mesh: wide: 32 (over x_hi, z, core), narrow: 8 (over y, x_lo).
Axes of the slice: x: 4 (x_hi: 2, x_lo: 2; x = x_hi * 2 + x_lo), y: 4, z: 8, core: 2. Of those that a mesh axis runs over, the one named last changes fastest.
Arguments:
- embeddings: bfloat16 [131072, 1024], P(('wide', 'narrow')), may hold values from -6 to 6
- projection: bfloat16 [1024, 256], replicated, may hold values from -0.1875 to 0.1875
- cluster_id: int32 [131072], P(('wide', 'narrow')), may hold values from 0 to 15, never falling along the last dimension, each value on 1 to 16384 neighbouring positions
Outputs:
- best_match: float32 [131072], P('wide')
The draws below stay inside these ranges and needn't reach their ends.
Inputs may be any that keep to these rules, and one draw needn't show every extreme that they name: cluster_id never falls along the rows; each cluster holds 1 to 16384 rows, one exactly 16384.
All inputs are finite; a program needn't handle non-finite values.
Results may differ from the reference program's by a relative error of at most 0.00089.
Values may be sent and summed in bfloat16 or wider, within the bound.
A program may use at most 64 MiB of HBM per device.

```python
import math
import jax
import jax.numpy as jnp
import numpy as np
from jax import lax

D = 1024
SK = 256
BLOCK = 4096
ROWS = 131072
CLUSTERS = 16
SPAN = 16384


def shard_levels(key, shape, split, least, top_value):
    factor_of = 1.0
    for axis_at, parts in split:
        steps = jax.random.uniform(jax.random.fold_in(jax.random.fold_in(key, 6), axis_at), (parts,), jnp.float32, least / len(split), top_value / len(split))
        factor_of = factor_of * jnp.repeat(jnp.exp(steps), shape[axis_at] // parts).reshape((-1,) + (1,) * (len(shape) - 1 - axis_at))
    return factor_of


def length_profile(number_of, total, limit, lean):
    portions = [(1 << 20) // math.isqrt(standing ** lean) + 1 for standing in range(2, number_of + 1)]
    spare, holding = total - limit - (number_of - 1), [1] * (number_of - 1)
    while spare > 0:
        free = [i for i in range(number_of - 1) if holding[i] < limit]
        whole, budget = sum([portions[i] for i in free]), spare
        for i in free:
            addition = min(limit - holding[i], max(1, budget * portions[i] // whole), spare)
            holding[i] = holding[i] + addition
            spare = spare - addition
    return np.array([limit] + holding)


def uneven_parts(rng, amount, total, most, skew):
    if amount == 2:
        one = jax.random.randint(rng, (), max(1, total - most), min(most, total - 1) + 1)
        return jnp.stack([one, total - one])
    sizes = jnp.asarray(length_profile(amount, total, most, skew), jnp.int32)
    twos = (amount - 1) // 2
    source_of, sink = sizes[1:1 + 2 * twos:2], sizes[2:2 + 2 * twos:2]
    slack = jnp.minimum(source_of - 1, most - sink)
    shifted = jax.random.randint(jax.random.fold_in(rng, 1), (twos,), 0, 1 << 20) % (slack + 1)
    sizes = sizes.at[1:1 + 2 * twos:2].set(source_of - shifted).at[2:2 + 2 * twos:2].set(sink + shifted)
    return sizes[jax.random.permutation(jax.random.fold_in(rng, 2), amount)]


def centred(rng, shape, spread, most, cuts=(), kind=jnp.bfloat16):
    array = jax.random.normal(rng, shape, jnp.float32) * spread
    if len(cuts) > 0:
        array = shard_levels(rng, shape, cuts, -0.22, 0.18) * array
    return jnp.clip(array, min=-most, max=most).astype(kind)


def setup_inputs(seed: int = 0) -> dict:
    key_of = jax.random.split(jax.random.key(seed), 4)
    embeddings = centred(key_of[0], (ROWS, D), 1.0, 6.0, ((0, 256),))
    projection = centred(key_of[1], (D, SK), D ** -0.5, 0.1875)
    cluster_id = jnp.searchsorted(jnp.cumsum(uneven_parts(key_of[2], CLUSTERS, ROWS, SPAN, 2)), jnp.arange(ROWS), side="right").astype(jnp.int32)
    return dict(embeddings=embeddings, projection=projection, cluster_id=cluster_id)


def reference(embeddings, projection, cluster_id):
    sketch = jnp.dot(embeddings, projection, preferred_element_type=jnp.float32)
    squares = lax.optimization_barrier(jnp.sum(sketch * sketch, axis=1, keepdims=True))
    inverse = lax.rsqrt(squares + 1e-06)
    unit = (sketch * inverse).astype(jnp.bfloat16)
    blocks = ROWS // BLOCK
    unit_blocks = unit.reshape(blocks, BLOCK, SK)
    id_blocks = cluster_id.reshape(blocks, BLOCK)

    def one_block(index):
        queries = unit_blocks[index]
        query_ids = id_blocks[index]
        best = jnp.full((BLOCK,), -1.0, jnp.float32)
        for offset in (1, 2, -1, -2):
            other = (index - offset) % blocks
            keys = unit_blocks[other]
            key_ids = id_blocks[other]
            scores = jnp.dot(queries, keys.T, preferred_element_type=jnp.float32)
            same = query_ids[:, None] == key_ids[None, :]
            best = jnp.maximum(best, lax.optimization_barrier(jnp.max(jnp.where(same, scores, jnp.float32(-1.0)), axis=1)))
        return best
    result = lax.map(one_block, jnp.arange(blocks, dtype=jnp.int32))
    return result.reshape(ROWS)
```

```python
import jax
import jax.numpy as jnp
from jax import lax
from jax.experimental import pallas as pl
from jax.experimental.pallas import tpu as pltpu
from jax.sharding import PartitionSpec as P

MESH = pl.DeviceIdType.MESH
ROWS = 512
SK = 256
D = 1024
CHUNKS = 2
CH = ROWS // CHUNKS
PLANES = 16
LANES = 128
GROUPS = ROWS // LANES


def device(plane, n, core):
    return (lax.rem(plane + PLANES, PLANES) * 2 + core, n)


def kernel(
    emb,
    proj,
    ids,
    out,
    emb_v,
    proj_v,
    r_unit,
    s_unit,
    r_ids,
    s_ids,
    r_col,
    row_acc,
    col_acc,
    row_all,
    col_src,
    col_all,
    in_sem,
    y_send,
    r_recv,
    s_send,
    s_recv,
    f_send,
    id_send,
    rid_recv,
    sid_recv,
    tail_send,
    tail_recv,
):
    wide, n = lax.axis_index("wide"), lax.axis_index("narrow")
    plane, core = wide // 2, lax.rem(wide, 2)
    y, x = n // 2, lax.rem(n, 2)
    n_x = y * 2 + 1 - x

    proj_in = pltpu.make_async_copy(proj, proj_v, in_sem.at[CHUNKS])
    proj_in.start()
    emb_in = []
    for k in range(CHUNKS):
        rows = pl.ds(k * CH, CH)
        emb_in.append(pltpu.make_async_copy(emb.at[rows], emb_v.at[rows], in_sem.at[k]))
        emb_in[k].start()

    barrier = pltpu.get_barrier_semaphore()

    def greet(where):
        pl.semaphore_signal(barrier, inc=1, device_id=where, device_id_type=MESH)

    for k in range(1, 8):
        greet(device(plane, lax.rem(n + k, 8), core))
    for k in range(8):
        greet(device(plane - 1 + core, k, 0))
        greet(device(plane - 1 + 2 * core, k, 1))
    for m in (n, n_x):
        greet(device(plane + 1, m, 0))
        greet(device(plane - core, m, 1))

    def y_peer(k):
        return device(plane, lax.rem(y + k, 4) * 2 + x, core)

    def unit_copy(k, to_slot, buf, send, recv, where):
        rows = pl.ds(k * CH, CH)
        return pltpu.make_async_remote_copy(
            src_ref=r_unit.at[0, rows],
            dst_ref=buf.at[to_slot, rows],
            send_sem=send,
            recv_sem=recv.at[to_slot, k],
            device_id=where,
            device_id_type=MESH,
        )

    def y_copies(k):
        return [
            unit_copy(k, 4 - d, r_unit, y_send.at[d - 1, k], r_recv, y_peer(d))
            for d in (2, 1, 3)
        ]

    def s_copies_0(k):
        return [
            unit_copy(k, 3, s_unit, s_send.at[1, k], s_recv, device(plane - 1, n_x, 0)),
            unit_copy(k, 2, s_unit, s_send.at[0, k], s_recv, device(plane - 1, n, 0)),
        ]

    def s_copies_1(k):
        return [
            unit_copy(k, 1, s_unit, s_send.at[3, k], s_recv, device(plane + 1, n_x, 1)),
            unit_copy(k, 0, s_unit, s_send.at[2, k], s_recv, device(plane + 1, n, 1)),
            unit_copy(k, 1, s_unit, s_send.at[1, k], s_recv, device(plane, n_x, 0)),
            unit_copy(k, 0, s_unit, s_send.at[0, k], s_recv, device(plane, n, 0)),
        ]

    def id_copy(to_slot, buf, send, recv, where):
        return pltpu.make_async_remote_copy(
            src_ref=ids,
            dst_ref=buf.at[to_slot],
            send_sem=send,
            recv_sem=recv.at[to_slot],
            device_id=where,
            device_id_type=MESH,
        )

    def id_copies_y():
        return [id_copy(4 - d, r_ids, id_send.at[d - 1], rid_recv, y_peer(d)) for d in (2, 1, 3)]

    def id_copies_0():
        return [
            id_copy(slot, s_ids, id_send.at[3 + 2 * c + i], sid_recv, device(plane - 1, m, c))
            for c in (0, 1)
            for i, (slot, m) in enumerate(((2, n), (3, n_x)))
        ]

    def id_copies_1():
        return [
            id_copy(slot, s_ids, id_send.at[3 + 2 * c + i], sid_recv, device(plane + c, m, c))
            for c in (0, 1)
            for i, (slot, m) in enumerate(((0, n), (1, n_x)))
        ]

    def start(copies):
        for copy in copies:
            copy.start()

    def by_core(of_0, of_1, act):
        @pl.when(core == 0)
        def _():
            for copy in of_0():
                act(copy)

        @pl.when(core == 1)
        def _():
            for copy in of_1():
                act(copy)

    proj_in.wait()
    for k in range(CHUNKS):
        emb_in[k].wait()
        sketch = jnp.dot(
            emb_v[k * CH : (k + 1) * CH, :], proj_v[...], preferred_element_type=jnp.float32
        )
        squares = jnp.sum(sketch * sketch, axis=1, keepdims=True)
        unit = (sketch * lax.rsqrt(squares + 1e-06)).astype(jnp.bfloat16)
        r_unit[0, k * CH : (k + 1) * CH, :] = unit
        if k == 0:
            pl.semaphore_wait(barrier, 27)
        start(y_copies(k))
        by_core(lambda: s_copies_0(k), lambda: s_copies_1(k), lambda c: c.start())
        if k == 0:
            start(id_copies_y())
            by_core(id_copies_0, id_copies_1, lambda c: c.start())

    def columns(slot, rows):
        for j in range(GROUPS):
            row = rows[j : j + 1, :].astype(jnp.float32)
            r_col[slot, j * LANES : (j + 1) * LANES, :] = jnp.broadcast_to(row, (LANES, LANES)).T

    columns(0, ids[...])
    row_acc[...] = jnp.full_like(row_acc, -1.0)
    col_acc[...] = jnp.full_like(col_acc, -1.0)

    def tiles(r, k, slots):
        rows = pl.ds(pl.multiple_of(k * CH, CH), CH)
        a = r_unit[r, rows, :]
        a_ids = r_col[r, rows, :]
        best = row_acc[rows, :]
        for s in slots:
            scores = lax.dot_general(
                a, s_unit[s], (((1,), (1,)), ((), ())), preferred_element_type=jnp.float32
            )
            for j in range(GROUPS):
                lanes = slice(j * LANES, (j + 1) * LANES)
                b_ids = s_ids[s, j : j + 1, :].astype(jnp.float32)
                kept = jnp.where(a_ids == b_ids, scores[:, lanes], -1.0)
                best = jnp.maximum(best, kept)
                peak = jnp.max(kept.reshape(CH // 8, 8, LANES), axis=0)
                col_acc[s, :, lanes] = jnp.maximum(col_acc[s, :, lanes], peak)
        row_acc[rows, :] = best

    def rows_done(r):
        y_abs = lax.rem(y + r, 4)
        for j in range(GROUPS):
            part = row_acc[j * LANES : (j + 1) * LANES, :].T
            row_all[n, y_abs, j : j + 1, :] = jnp.max(part, axis=0, keepdims=True)
        if r != 2:
            row_acc[...] = jnp.full_like(row_acc, -1.0)

    def s_wait(s, k):
        rows = pl.ds(k * CH, CH)
        pltpu.make_async_copy(s_unit.at[s, rows], s_unit.at[s, rows], s_recv.at[s, k]).wait()

    def forward(s, k):
        rows = pl.ds(k * CH, CH)
        return pltpu.make_async_remote_copy(
            src_ref=s_unit.at[s, rows],
            dst_ref=s_unit.at[s, rows],
            send_sem=f_send.at[s - 2, k],
            recv_sem=s_recv.at[s, k],
            device_id=device(plane, n, 1),
            device_id_type=MESH,
        )

    def id_wait(buf, slot, recv):
        pltpu.make_async_copy(buf.at[slot], buf.at[slot], recv.at[slot]).wait()

    for s in range(4):
        id_wait(s_ids, s, sid_recv)
        for k in range(CHUNKS):
            s_wait(s, k)
            if s >= 2:

                @pl.when(core == 0)
                def _():
                    forward(s, k).start()

        @pl.loop(0, CHUNKS)
        def _(k):
            tiles(0, k, (s,))

    rows_done(0)
    for r in (1, 3, 2):
        id_wait(r_ids, r, rid_recv)
        columns(r, r_ids[r])

        @pl.loop(0, CHUNKS)
        def _(k):
            rows = pl.ds(pl.multiple_of(k * CH, CH), CH)
            pltpu.make_async_copy(r_unit.at[r, rows], r_unit.at[r, rows], r_recv.at[r, k]).wait()
            tiles(r, k, range(4))

        rows_done(r)

    for s in range(4):
        x_abs = x if s % 2 == 0 else 1 - x
        for j in range(GROUPS):
            col_src[s // 2, x_abs, j : j + 1, :] = jnp.max(
                col_acc[s, :, j * LANES : (j + 1) * LANES], axis=0, keepdims=True
            )

    def tail(src, dst, kind, where):
        return pltpu.make_async_remote_copy(
            src_ref=src,
            dst_ref=dst,
            send_sem=tail_send.at[kind],
            recv_sem=tail_recv.at[kind],
            device_id=where,
            device_id_type=MESH,
        )

    for k in range(8):
        tail(col_src.at[1], col_all.at[core, n], 1, device(plane + 1, k, 0)).start()
    for k in range(8):
        tail(col_src.at[0], col_all.at[core, n], 1, device(plane - core, k, 1)).start()
    for k in range(1, 8):
        tail(row_all.at[n], row_all.at[n], 0, device(plane, lax.rem(n + k, 8), core)).start()

    some = row_all.at[pl.ds(0, 7)]
    pltpu.make_async_copy(some, some, tail_recv.at[0]).wait()
    pltpu.make_async_copy(col_all, col_all, tail_recv.at[1]).wait()
    for y_abs in range(4):
        for x_abs in range(2):
            best = jnp.full((GROUPS, LANES), -1.0, jnp.float32)
            for y_from in range(4):
                best = jnp.maximum(best, row_all[y_from * 2 + x_abs, y_abs])
            for c in range(2):
                for x_from in range(2):
                    best = jnp.maximum(best, col_all[c, y_abs * 2 + x_from, x_abs])
            out[y_abs * 2 + x_abs] = best

    pltpu.make_async_copy(some, some, tail_send.at[0]).wait()
    pltpu.make_async_copy(col_all, col_all, tail_send.at[1]).wait()
    for k in range(CHUNKS):
        for copy in y_copies(k):
            copy.wait_send()
        by_core(lambda: s_copies_0(k), lambda: s_copies_1(k), lambda c: c.wait_send())
        for s in (2, 3):

            @pl.when(core == 0)
            def _():
                forward(s, k).wait_send()

    for copy in id_copies_y():
        copy.wait_send()
    by_core(id_copies_0, id_copies_1, lambda c: c.wait_send())


def body(embeddings, projection, cluster_id):
    dma = pltpu.SemaphoreType.DMA
    best = pl.pallas_call(
        kernel,
        out_shape=jax.ShapeDtypeStruct((8, GROUPS, LANES), jnp.float32),
        in_specs=[
            pl.BlockSpec(memory_space=pl.ANY),
            pl.BlockSpec(memory_space=pl.ANY),
            pl.BlockSpec(memory_space=pltpu.VMEM),
        ],
        out_specs=pl.BlockSpec(memory_space=pltpu.VMEM),
        scratch_shapes=[
            pltpu.VMEM((ROWS, D), jnp.bfloat16),
            pltpu.VMEM((D, SK), jnp.bfloat16),
            pltpu.VMEM((4, ROWS, SK), jnp.bfloat16),
            pltpu.VMEM((4, ROWS, SK), jnp.bfloat16),
            pltpu.VMEM((4, GROUPS, LANES), jnp.int32),
            pltpu.VMEM((4, GROUPS, LANES), jnp.int32),
            pltpu.VMEM((4, ROWS, LANES), jnp.float32),
            pltpu.VMEM((ROWS, LANES), jnp.float32),
            pltpu.VMEM((4, 8, ROWS), jnp.float32),
            pltpu.VMEM((8, 4, GROUPS, LANES), jnp.float32),
            pltpu.VMEM((2, 2, GROUPS, LANES), jnp.float32),
            pltpu.VMEM((2, 8, 2, GROUPS, LANES), jnp.float32),
            dma((CHUNKS + 1,)),
            dma((3, CHUNKS)),
            dma((4, CHUNKS)),
            dma((4, CHUNKS)),
            dma((4, CHUNKS)),
            dma((2, CHUNKS)),
            dma((7,)),
            dma((4,)),
            dma((4,)),
            dma((2,)),
            dma((2,)),
        ],
        compiler_params=pltpu.CompilerParams(
            collective_id=0, has_side_effects=True, vmem_limit_bytes=62 << 20
        ),
        name="best_match",
    )(embeddings, projection, cluster_id.reshape(GROUPS, LANES))
    return best.reshape(8 * ROWS)


def solution(mesh):
    in_specs = (P(("wide", "narrow"), None), P(), P(("wide", "narrow")))
    out_specs = P("wide")
    return jax.shard_map(body, mesh=mesh, in_specs=in_specs, out_specs=out_specs, check_vma=False)
```

```python
import jax
import jax.numpy as jnp
from jax import lax
from jax.experimental import pallas as pl
from jax.experimental.pallas import tpu as pltpu
from jax.sharding import PartitionSpec as P

MESH = pl.DeviceIdType.MESH
ROWS = 512
SK = 256
D = 1024
CHUNKS = 4
CH = ROWS // CHUNKS
HALF = ROWS // 2
PLANES = 16
LANES = 128
GROUPS = ROWS // LANES


def device(plane, n, core):
    return (lax.rem(plane + PLANES, PLANES) * 2 + core, n)


def kernel(
    emb,
    proj,
    ids,
    out,
    emb_v,
    proj_v,
    r_unit,
    s_unit,
    r_ids,
    s_ids,
    r_col,
    row_acc,
    col_acc,
    row_all,
    col_src,
    col_all,
    in_sem,
    y_send,
    relay_send,
    r_recv,
    p_send,
    f_send,
    q_send,
    s_recv,
    id_send,
    rid_recv,
    sid_recv,
    tail_send,
    tail_recv,
):
    wide, n = lax.axis_index("wide"), lax.axis_index("narrow")
    plane, core = wide // 2, lax.rem(wide, 2)
    y, x = n // 2, lax.rem(n, 2)
    n_x = y * 2 + 1 - x
    crosses_out = lax.rem(plane, 8) == 7
    crosses_in = lax.rem(plane, 8) == 0
    n_p = jnp.where(crosses_out, n_x, n)
    n_f = jnp.where(crosses_out, n, n_x)
    x_p = jnp.where(crosses_in, 1 - x, x)
    x_q = jnp.where(core == 0, x_p, x)

    proj_in = pltpu.make_async_copy(proj, proj_v, in_sem.at[2])
    proj_in.start()
    emb_in = []
    for h in range(2):
        rows = pl.ds(h * HALF, HALF)
        emb_in.append(pltpu.make_async_copy(emb.at[rows], emb_v.at[rows], in_sem.at[h]))
        emb_in[h].start()

    barrier = pltpu.get_barrier_semaphore()

    def greet(where):
        pl.semaphore_signal(barrier, inc=1, device_id=where, device_id_type=MESH)

    for m in (n, n_x):
        greet(device(plane - 1, m, core))
        greet(device(plane - 1 + core, m, 1 - core))
    for k in range(1, 8):
        greet(device(plane, lax.rem(n + k, 8), core))
    for k in range(8):
        greet(device(plane + 1, k, core))
        greet(device(plane + core, k, 1 - core))

    def remote(src, dst, send, recv, where):
        return pltpu.make_async_remote_copy(
            src_ref=src,
            dst_ref=dst,
            send_sem=send,
            recv_sem=recv,
            device_id=where,
            device_id_type=MESH,
        )

    def piece(k):
        return pl.ds(k * CH, CH)

    def y_peer(d):
        return device(plane, lax.rem(y + d, 4) * 2 + x, core)

    def y_copy(d, k):
        src, dst = r_unit.at[0, piece(k)], r_unit.at[4 - d, piece(k)]
        return remote(src, dst, y_send.at[d // 2, k], r_recv.at[4 - d, k], y_peer(d))

    def relay_copy(d, k):
        src, dst = r_unit.at[d, piece(k)], r_unit.at[2, piece(k)]
        return remote(src, dst, relay_send.at[d // 2, k % 2], r_recv.at[2, k], y_peer(4 - d))

    def p_copy(k):
        src, dst = r_unit.at[0, piece(k)], s_unit.at[0, piece(k)]
        return remote(src, dst, p_send.at[k], s_recv.at[0, k], device(plane + 1, n_p, core))

    def f_copy(k):
        src, dst = s_unit.at[0, piece(k)], s_unit.at[1, piece(k)]
        return remote(src, dst, f_send.at[k], s_recv.at[1, k], device(plane, n_x, core))

    def q0_copy(i, k):
        src, dst = r_unit.at[0, piece(k)], s_unit.at[2 + i, piece(k)]
        where = device(plane, n_x if i else n, 1)
        return remote(src, dst, q_send.at[i, k], s_recv.at[2 + i, k], where)

    def q1_copy(i, k):
        src, dst = s_unit.at[i, piece(k)], s_unit.at[2 + i, piece(k)]
        return remote(src, dst, q_send.at[i, k], s_recv.at[2 + i, k], device(plane, n, 0))

    def id_copies():
        copies = [
            remote(ids, r_ids.at[4 - d], id_send.at[d - 1], rid_recv.at[4 - d], y_peer(d))
            for d in (2, 1, 3)
        ]
        n_q = jnp.where(core == 0, n, n_p)
        n_r = jnp.where(core == 0, n_x, n_f)
        for slot, where in enumerate(
            (
                device(plane + 1, n_p, core),
                device(plane + 1, n_f, core),
                device(plane + core, n_q, 1 - core),
                device(plane + core, n_r, 1 - core),
            )
        ):
            copies.append(remote(ids, s_ids.at[slot], id_send.at[3 + slot], sid_recv.at[slot], where))
        return copies

    proj_in.wait()
    for h in range(2):
        emb_in[h].wait()
        rows = slice(h * HALF, (h + 1) * HALF)
        sketch = jnp.dot(emb_v[rows, :], proj_v[...], preferred_element_type=jnp.float32)
        squares = jnp.sum(sketch * sketch, axis=1, keepdims=True)
        r_unit[0, rows, :] = (sketch * lax.rsqrt(squares + 1e-06)).astype(jnp.bfloat16)
        if h == 0:
            pl.semaphore_wait(barrier, 27)
        near = (2 * h, 2 * h + 1)
        for k in near:
            p_copy(k).start()
            y_copy(1, k).start()
            if h == 1:
                y_copy(3, k).start()

        @pl.when(core == 0)
        def _():
            for k in near:
                q0_copy(1, k).start()
                q0_copy(0, k).start()

        if h == 0:
            y_copy(3, 0).start()
            for copy in id_copies():
                copy.start()
        else:
            y_copy(3, 1).start()

    def columns(slot, rows):
        for j in range(GROUPS):
            row = rows[j : j + 1, :].astype(jnp.float32)
            r_col[slot, j * LANES : (j + 1) * LANES, :] = jnp.broadcast_to(row, (LANES, LANES)).T

    columns(0, ids[...])
    row_acc[...] = jnp.full_like(row_acc, -1.0)
    col_acc[...] = jnp.full_like(col_acc, -1.0)

    def landed(ref, sem):
        pltpu.make_async_copy(ref, ref, sem).wait()

    def r_wait(d, k):
        landed(r_unit.at[d, piece(k)], r_recv.at[d, k])

    def s_wait(s, k):
        landed(s_unit.at[s, piece(k)], s_recv.at[s, k])

    def to_core_0(i, k):
        @pl.when(core == 1)
        def _():
            q1_copy(i, k).start()

    for k in range(CHUNKS):
        if k < 2:
            for d, piece_of in ((1, 2 + k), (3, k)):
                r_wait(d, piece_of)
                relay_copy(d, piece_of).start()
        s_wait(0, k)
        f_copy(k).start()
        to_core_0(0, k)

    for d in (1, 3, 2):
        landed(r_ids.at[d], rid_recv.at[d])
        columns(d, r_ids[d])
    for s in range(4):
        landed(s_ids.at[s], sid_recv.at[s])
    for k in range(2):
        r_wait(1, k)
        r_wait(3, 2 + k)

    def tiles(s, blocks, where):
        def step(b, peaks):
            r, rows = where(b)
            scores = lax.dot_general(
                r_unit[r, rows, :],
                s_unit[s],
                (((1,), (1,)), ((), ())),
                preferred_element_type=jnp.float32,
            )
            a_ids = r_col[r, rows, :]
            best = row_acc[r, rows, :]
            new = []
            for j in range(GROUPS):
                b_ids = s_ids[s, j : j + 1, :].astype(jnp.float32)
                kept = jnp.where(a_ids == b_ids, scores[:, j * LANES : (j + 1) * LANES], -1.0)
                best = jnp.maximum(best, kept)
                peak = jnp.max(kept.reshape(HALF // 8, 8, LANES), axis=0)
                new.append(jnp.maximum(peaks[j], peak))
            row_acc[r, rows, :] = best
            return tuple(new)

        peaks = tuple(col_acc[s, j] for j in range(GROUPS))
        peaks = lax.fori_loop(0, blocks, step, peaks)
        for j in range(GROUPS):
            col_acc[s, j] = peaks[j]

    def rows_of(b):
        return pl.ds(pl.multiple_of(lax.rem(b, 2) * HALF, HALF), HALF)

    def near_blocks(b):
        t = b // 2
        return t + t // 2, rows_of(b)

    def far_blocks(b):
        return 2, rows_of(b)

    def all_blocks(b):
        return b // 2, rows_of(b)

    def slot(of_0, of_1):
        return jnp.where(core == 0, of_0, of_1)

    def s_wait_all(s):
        for k in range(CHUNKS):
            s_wait(s, k)

    @pl.when(core == 1)
    def _():
        s_wait_all(2)

    tiles(slot(0, 2), 6, near_blocks)

    @pl.when(core == 0)
    def _():
        s_wait_all(2)

    @pl.when(core == 1)
    def _():
        s_wait_all(3)
        for k in (0, 1):
            s_wait(1, k)
            q1_copy(1, k).start()

    tiles(slot(2, 3), 6, near_blocks)

    for k in range(CHUNKS):
        r_wait(2, k)

    @pl.when(core == 1)
    def _():
        for k in (2, 3):
            s_wait(1, k)
            q1_copy(1, k).start()

    tiles(slot(0, 2), 2, far_blocks)
    tiles(slot(2, 3), 2, far_blocks)

    @pl.when(core == 0)
    def _():
        s_wait_all(1)

    tiles(slot(1, 0), 8, all_blocks)

    @pl.when(core == 0)
    def _():
        s_wait_all(3)

    tiles(slot(3, 1), 8, all_blocks)

    for s in range(4):
        x_abs = (x_p, 1 - x_p, x_q, 1 - x_q)[s]
        for j in range(GROUPS):
            col_src[s // 2, x_abs, j : j + 1, :] = jnp.max(col_acc[s, j], axis=0, keepdims=True)

    def tail(src, dst, kind, where):
        return remote(src, dst, tail_send.at[kind], tail_recv.at[kind], where)

    for k in range(8):
        tail(col_src.at[0], col_all.at[0, n], 1, device(plane - 1, k, core)).start()
        tail(col_src.at[1], col_all.at[1, n], 1, device(plane - 1 + core, k, 1 - core)).start()

    for r in range(4):
        y_abs = lax.rem(y + r, 4)
        for j in range(GROUPS):
            part = row_acc[r, j * LANES : (j + 1) * LANES, :].T
            row_all[n, y_abs, j : j + 1, :] = jnp.max(part, axis=0, keepdims=True)
    for k in range(1, 8):
        tail(row_all.at[n], row_all.at[n], 0, device(plane, lax.rem(n + k, 8), core)).start()

    some = row_all.at[pl.ds(0, 7)]
    landed(some, tail_recv.at[0])
    landed(col_all, tail_recv.at[1])
    for y_abs in range(4):
        for x_abs in range(2):
            best = jnp.full((GROUPS, LANES), -1.0, jnp.float32)
            for y_from in range(4):
                best = jnp.maximum(best, row_all[y_from * 2 + x_abs, y_abs])
            for g in range(2):
                for x_from in range(2):
                    best = jnp.maximum(best, col_all[g, y_abs * 2 + x_from, x_abs])
            out[y_abs * 2 + x_abs] = best

    landed(some, tail_send.at[0])
    landed(col_all, tail_send.at[1])
    for k in range(CHUNKS):
        y_copy(1, k).wait_send()
        y_copy(3, k).wait_send()
        relay_copy(1 if k >= 2 else 3, k).wait_send()
        p_copy(k).wait_send()
        f_copy(k).wait_send()
        for i in range(2):
            landed(r_unit.at[0, piece(k)], q_send.at[i, k])
    for copy in id_copies():
        copy.wait_send()


def body(embeddings, projection, cluster_id):
    dma = pltpu.SemaphoreType.DMA
    best = pl.pallas_call(
        kernel,
        out_shape=jax.ShapeDtypeStruct((8, GROUPS, LANES), jnp.float32),
        in_specs=[
            pl.BlockSpec(memory_space=pl.ANY),
            pl.BlockSpec(memory_space=pl.ANY),
            pl.BlockSpec(memory_space=pltpu.VMEM),
        ],
        out_specs=pl.BlockSpec(memory_space=pltpu.VMEM),
        scratch_shapes=[
            pltpu.VMEM((ROWS, D), jnp.bfloat16),
            pltpu.VMEM((D, SK), jnp.bfloat16),
            pltpu.VMEM((4, ROWS, SK), jnp.bfloat16),
            pltpu.VMEM((4, ROWS, SK), jnp.bfloat16),
            pltpu.VMEM((4, GROUPS, LANES), jnp.int32),
            pltpu.VMEM((4, GROUPS, LANES), jnp.int32),
            pltpu.VMEM((4, ROWS, LANES), jnp.float32),
            pltpu.VMEM((4, ROWS, LANES), jnp.float32),
            pltpu.VMEM((4, GROUPS, 8, LANES), jnp.float32),
            pltpu.VMEM((8, 4, GROUPS, LANES), jnp.float32),
            pltpu.VMEM((2, 2, GROUPS, LANES), jnp.float32),
            pltpu.VMEM((2, 8, 2, GROUPS, LANES), jnp.float32),
            dma((3,)),
            dma((2, CHUNKS)),
            dma((2, 2)),
            dma((4, CHUNKS)),
            dma((CHUNKS,)),
            dma((CHUNKS,)),
            dma((2, CHUNKS)),
            dma((4, CHUNKS)),
            dma((7,)),
            dma((4,)),
            dma((4,)),
            dma((2,)),
            dma((2,)),
        ],
        compiler_params=pltpu.CompilerParams(
            collective_id=0, has_side_effects=True, vmem_limit_bytes=62 << 20
        ),
        name="best_match",
    )(embeddings, projection, cluster_id.reshape(GROUPS, LANES))
    return best.reshape(8 * ROWS)


def solution(mesh):
    in_specs = (P(("wide", "narrow"), None), P(), P(("wide", "narrow")))
    out_specs = P("wide")
    return jax.shard_map(body, mesh=mesh, in_specs=in_specs, out_specs=out_specs, check_vma=False)
```

```python
import jax
import jax.numpy as jnp
from jax import lax
from jax.experimental import pallas as pl
from jax.experimental.pallas import tpu as pltpu
from jax.sharding import PartitionSpec as P

MESH = pl.DeviceIdType.MESH
ROWS = 512
SK = 256
D = 1024
CHUNKS = 4
CH = ROWS // CHUNKS
HALF = ROWS // 2
PLANES = 16
LANES = 128
GROUPS = ROWS // LANES


def device(plane, n, core):
    return (lax.rem(plane + PLANES, PLANES) * 2 + core, n)


def kernel(
    emb,
    proj,
    ids_in,
    out,
    emb_v,
    proj_v,
    ids,
    r_unit,
    s_unit,
    r_ids,
    s_ids,
    r_col,
    row_acc,
    col_acc,
    row_all,
    col_src,
    col_all,
    in_sem,
    y_send,
    relay_send,
    r_recv,
    p_send,
    f_send,
    q_send,
    s_recv,
    id_send,
    rid_recv,
    sid_recv,
    tail_send,
    tail_recv,
):
    wide, n = lax.axis_index("wide"), lax.axis_index("narrow")
    plane, core = wide // 2, lax.rem(wide, 2)
    y, x = n // 2, lax.rem(n, 2)
    n_x = y * 2 + 1 - x
    crosses_out = lax.rem(plane, 8) == 7
    crosses_in = lax.rem(plane, 8) == 0
    n_p = jnp.where(crosses_out, n_x, n)
    n_f = jnp.where(crosses_out, n, n_x)
    x_p = jnp.where(crosses_in, 1 - x, x)
    p_slot, f_slot = 2 * core, 2 + core

    proj_in = pltpu.make_async_copy(proj, proj_v, in_sem.at[2])
    proj_in.start()
    ids_copy = pltpu.make_async_copy(ids_in, ids, in_sem.at[3])
    emb_in = []
    for h in range(2):
        rows = pl.ds(h * HALF, HALF)
        emb_in.append(pltpu.make_async_copy(emb.at[rows], emb_v.at[rows], in_sem.at[h]))
        emb_in[h].start()
    ids_copy.start()

    barrier = pltpu.get_barrier_semaphore()

    def greet(where):
        pl.semaphore_signal(barrier, inc=1, device_id=where, device_id_type=MESH)

    for m in (n, n_x):
        greet(device(plane - 1, m, core))
        greet(device(plane - 1 + core, m, 1 - core))
    for k in range(1, 8):
        greet(device(plane, lax.rem(n + k, 8), core))
    for k in range(8):
        greet(device(plane + 1, k, core))
        greet(device(plane + core, k, 1 - core))

    def remote(src, dst, send, recv, where):
        return pltpu.make_async_remote_copy(
            src_ref=src,
            dst_ref=dst,
            send_sem=send,
            recv_sem=recv,
            device_id=where,
            device_id_type=MESH,
        )

    def piece(k):
        return pl.ds(k * CH, CH)

    def y_peer(d):
        return device(plane, lax.rem(y + d, 4) * 2 + x, core)

    def y_copy(d, k):
        slot = 2 if d == 1 else 1
        src, dst = r_unit.at[0, piece(k)], r_unit.at[slot, piece(k)]
        return remote(src, dst, y_send.at[slot - 1, k], r_recv.at[slot, k], y_peer(d))

    def relay_copy(slot, k):
        src, dst = r_unit.at[slot, piece(k)], r_unit.at[3, piece(k)]
        where = y_peer(3 if slot == 1 else 1)
        return remote(src, dst, relay_send.at[slot - 1, k % 2], r_recv.at[3, k], where)

    def p_copy(k):
        src, dst = r_unit.at[0, piece(k)], s_unit.at[p_slot, piece(k)]
        return remote(src, dst, p_send.at[k], s_recv.at[p_slot, k], device(plane + 1, n_p, core))

    def f_copy(k):
        src, dst = s_unit.at[p_slot, piece(k)], s_unit.at[f_slot, piece(k)]
        return remote(src, dst, f_send.at[k], s_recv.at[f_slot, k], device(plane, n_x, core))

    def q0_copy(i, k):
        src, dst = r_unit.at[0, piece(k)], s_unit.at[i, piece(k)]
        where = device(plane, n_x if i else n, 1)
        return remote(src, dst, q_send.at[i, k], s_recv.at[i, k], where)

    def q1_copy(i, k):
        src, dst = s_unit.at[2 + i, piece(k)], s_unit.at[1 + 2 * i, piece(k)]
        where = device(plane, n, 0)
        return remote(src, dst, q_send.at[i, k], s_recv.at[1 + 2 * i, k], where)

    def id_copies():
        copies = [
            remote(ids, r_ids.at[slot], id_send.at[slot - 1], rid_recv.at[slot], y_peer(d))
            for slot, d in ((3, 2), (2, 1), (1, 3))
        ]
        n_q = jnp.where(core == 0, n, n_p)
        n_r = jnp.where(core == 0, n_x, n_f)
        for i, (slot, where) in enumerate(
            (
                (p_slot, device(plane + 1, n_p, core)),
                (f_slot, device(plane + 1, n_f, core)),
                (core, device(plane + core, n_q, 1 - core)),
                (1 + 2 * core, device(plane + core, n_r, 1 - core)),
            )
        ):
            copies.append(remote(ids, s_ids.at[slot], id_send.at[3 + i], sid_recv.at[slot], where))
        return copies

    proj_in.wait()
    for h in range(2):
        emb_in[h].wait()
        rows = slice(h * HALF, (h + 1) * HALF)
        sketch = jnp.dot(emb_v[rows, :], proj_v[...], preferred_element_type=jnp.float32)
        squares = jnp.sum(sketch * sketch, axis=1, keepdims=True)
        r_unit[0, rows, :] = (sketch * lax.rsqrt(squares + 1e-06)).astype(jnp.bfloat16)
        if h == 0:
            pl.semaphore_wait(barrier, 27)
        near = (2 * h, 2 * h + 1)
        for k in near:
            p_copy(k).start()
            y_copy(1, k).start()
            if h == 1:
                y_copy(3, k).start()

        @pl.when(core == 0)
        def _():
            for k in near:
                q0_copy(1, k).start()
                q0_copy(0, k).start()

        if h == 0:
            y_copy(3, 0).start()
            ids_copy.wait()
            for copy in id_copies():
                copy.start()
        else:
            y_copy(3, 1).start()

    def columns(slot, rows):
        for j in range(GROUPS):
            row = rows[j : j + 1, :].astype(jnp.float32)
            r_col[slot, j * LANES : (j + 1) * LANES, :] = jnp.broadcast_to(row, (LANES, LANES)).T

    columns(0, ids[...])
    row_acc[...] = jnp.full_like(row_acc, -1.0)
    col_acc[...] = jnp.full_like(col_acc, -1.0)

    def landed(ref, sem):
        pltpu.make_async_copy(ref, ref, sem).wait()

    def r_wait(d, k):
        landed(r_unit.at[d, piece(k)], r_recv.at[d, k])

    def s_wait(s, k):
        landed(s_unit.at[s, piece(k)], s_recv.at[s, k])

    def to_core_0(i, k):
        @pl.when(core == 1)
        def _():
            q1_copy(i, k).start()

    for k in range(CHUNKS):
        if k < 2:
            for slot, piece_of in ((1, 2 + k), (2, k)):
                r_wait(slot, piece_of)
                relay_copy(slot, piece_of).start()
        s_wait(p_slot, k)
        f_copy(k).start()
        to_core_0(0, k)

    for slot in (1, 2, 3):
        landed(r_ids.at[slot], rid_recv.at[slot])
        columns(slot, r_ids[slot])
    for s in range(4):
        landed(s_ids.at[s], sid_recv.at[s])
    for k in range(2):
        r_wait(1, k)
        r_wait(2, 2 + k)

    def score(r, s, peaks, bests):
        scores = lax.dot_general(
            r_unit[r], s_unit[s], (((1,), (1,)), ((), ())), preferred_element_type=jnp.float32
        )
        a_ids = r_col[r]
        for j in range(GROUPS):
            b_ids = s_ids[s, pl.ds(j, 1), :].astype(jnp.float32)
            kept = jnp.where(a_ids == b_ids, scores[:, j * LANES : (j + 1) * LANES], -1.0)
            bests[r] = jnp.maximum(bests[r], kept)
            peaks[j] = jnp.maximum(peaks[j], jnp.max(kept.reshape(ROWS // 8, 8, LANES), axis=0))

    @pl.loop(0, 4)
    def _(s):
        @pl.when(jnp.logical_and(s != p_slot, s != 4 - core))
        def _():
            for k in range(CHUNKS):
                s_wait(s, k)

        @pl.when(jnp.logical_and(core == 1, s > 0))
        def _():
            s_wait(3, s)
            q1_copy(1, s).start()

        @pl.when(jnp.logical_and(core == 1, s == 1))
        def _():
            s_wait(3, 0)
            q1_copy(1, 0).start()

        peaks = [col_acc[s, j] for j in range(GROUPS)]
        bests = {r: row_acc[r] for r in range(3)}
        for r in range(3):
            score(r, s, peaks, bests)
            row_acc[r] = bests[r]
        for j in range(GROUPS):
            col_acc[s, j] = peaks[j]

    def rows_done(r, best):
        at = lax.rem(y + (0, 1, 3, 2)[r], 4)
        for j in range(GROUPS):
            part = best[j * LANES : (j + 1) * LANES, :].T
            row_all[n, at, j : j + 1, :] = jnp.max(part, axis=0, keepdims=True)

    for k in range(CHUNKS):
        r_wait(3, k)
    bests = {3: row_acc[3]}
    for s in range(4):
        peaks = [col_acc[s, j] for j in range(GROUPS)]
        score(3, s, peaks, bests)
        block = jnp.where(core == 0, s % 2, 1 - s // 2)
        x_0 = x_p if s < 2 else 1 - x_p
        x_1 = (x, 1 - x, x_p, 1 - x_p)[s]
        x_abs = jnp.where(core == 0, x_0, x_1)
        for j in range(GROUPS):
            col_src[block, x_abs, j : j + 1, :] = jnp.max(peaks[j], axis=0, keepdims=True)
        if s < 3:
            rows_done(s, row_acc[s])

    def tail(src, dst, kind, where):
        return remote(src, dst, tail_send.at[kind], tail_recv.at[kind], where)

    for k in range(8):
        tail(col_src.at[0], col_all.at[0, n], 1, device(plane - 1, k, core)).start()
        tail(col_src.at[1], col_all.at[1, n], 1, device(plane - 1 + core, k, 1 - core)).start()

    rows_done(3, bests[3])
    for k in range(1, 8):
        tail(row_all.at[n], row_all.at[n], 0, device(plane, lax.rem(n + k, 8), core)).start()

    some = row_all.at[pl.ds(0, 7)]
    landed(some, tail_recv.at[0])
    landed(col_all, tail_recv.at[1])
    for y_abs in range(4):
        for x_abs in range(2):
            best = jnp.full((GROUPS, LANES), -1.0, jnp.float32)
            for y_from in range(4):
                best = jnp.maximum(best, row_all[y_from * 2 + x_abs, y_abs])
            for g in range(2):
                for x_from in range(2):
                    best = jnp.maximum(best, col_all[g, y_abs * 2 + x_from, x_abs])
            out[y_abs * 2 + x_abs] = best

    landed(some, tail_send.at[0])
    landed(col_all, tail_send.at[1])
    for k in range(CHUNKS):
        y_copy(1, k).wait_send()
        y_copy(3, k).wait_send()
        relay_copy(1 if k >= 2 else 2, k).wait_send()
        p_copy(k).wait_send()
        f_copy(k).wait_send()
        for i in range(2):
            landed(r_unit.at[0, piece(k)], q_send.at[i, k])
    for copy in id_copies():
        copy.wait_send()


def body(embeddings, projection, cluster_id):
    dma = pltpu.SemaphoreType.DMA
    best = pl.pallas_call(
        kernel,
        out_shape=jax.ShapeDtypeStruct((8, GROUPS, LANES), jnp.float32),
        in_specs=[
            pl.BlockSpec(memory_space=pltpu.HBM),
            pl.BlockSpec(memory_space=pltpu.HBM),
            pl.BlockSpec(memory_space=pltpu.HBM),
        ],
        out_specs=pl.BlockSpec(memory_space=pltpu.VMEM),
        scratch_shapes=[
            pltpu.VMEM((ROWS, D), jnp.bfloat16),
            pltpu.VMEM((D, SK), jnp.bfloat16),
            pltpu.VMEM((GROUPS, LANES), jnp.int32),
            pltpu.VMEM((4, ROWS, SK), jnp.bfloat16),
            pltpu.VMEM((4, ROWS, SK), jnp.bfloat16),
            pltpu.VMEM((4, GROUPS, LANES), jnp.int32),
            pltpu.VMEM((4, GROUPS, LANES), jnp.int32),
            pltpu.VMEM((4, ROWS, LANES), jnp.float32),
            pltpu.VMEM((4, ROWS, LANES), jnp.float32),
            pltpu.VMEM((4, GROUPS, 8, LANES), jnp.float32),
            pltpu.VMEM((8, 4, GROUPS, LANES), jnp.float32),
            pltpu.VMEM((2, 2, GROUPS, LANES), jnp.float32),
            pltpu.VMEM((2, 8, 2, GROUPS, LANES), jnp.float32),
            dma((4,)),
            dma((2, CHUNKS)),
            dma((2, 2)),
            dma((4, CHUNKS)),
            dma((CHUNKS,)),
            dma((CHUNKS,)),
            dma((2, CHUNKS)),
            dma((4, CHUNKS)),
            dma((7,)),
            dma((4,)),
            dma((4,)),
            dma((2,)),
            dma((2,)),
        ],
        compiler_params=pltpu.CompilerParams(
            collective_id=0, has_side_effects=True, vmem_limit_bytes=62 << 20
        ),
        name="best_match",
    )(embeddings, projection, cluster_id.reshape(GROUPS, LANES))
    return best.reshape(8 * ROWS)


def solution(mesh):
    in_specs = (P(("wide", "narrow"), None), P(), P(("wide", "narrow")))
    out_specs = P("wide")
    return jax.shard_map(body, mesh=mesh, in_specs=in_specs, out_specs=out_specs, check_vma=False)
```

```python
import jax
import jax.numpy as jnp
from jax import lax
from jax.experimental import pallas as pl
from jax.experimental.pallas import tpu as pltpu
from jax.sharding import PartitionSpec as P

MESH = pl.DeviceIdType.MESH
ROWS = 512
SK = 256
D = 1024
CHUNKS = 4
CH = ROWS // CHUNKS
HALF = ROWS // 2
HEAD = 16
PLANES = 16
LANES = 128
GROUPS = ROWS // LANES


def device(plane, n, core):
    return (lax.rem(plane + PLANES, PLANES) * 2 + core, n)


def kernel(
    emb,
    proj,
    ids_in,
    out,
    emb_v,
    proj_v,
    ids,
    r_unit,
    s_unit,
    r_col,
    row_acc,
    col_acc,
    row_all,
    col_src,
    col_all,
    in_sem,
    y_send,
    relay_send,
    r_recv,
    p_send,
    f_send,
    q_send,
    s_recv,
    tail_send,
    tail_recv,
    ready,
):
    wide, n = lax.axis_index("wide"), lax.axis_index("narrow")
    plane, core = wide // 2, lax.rem(wide, 2)
    y, x = n // 2, lax.rem(n, 2)
    n_x = y * 2 + 1 - x
    crosses_out = lax.rem(plane, 8) == 7
    crosses_in = lax.rem(plane, 8) == 0
    n_p = jnp.where(crosses_out, n_x, n)
    n_from = jnp.where(crosses_in, n_x, n)
    x_p = jnp.where(crosses_in, 1 - x, x)
    p_slot, f_slot = 2 * core, 2 + core

    proj_in = pltpu.make_async_copy(proj, proj_v, in_sem.at[2])
    proj_in.start()
    ids_copy = pltpu.make_async_copy(ids_in, ids, in_sem.at[3])
    emb_in = []
    for h in range(2):
        rows = pl.ds(h * HALF, HALF)
        emb_in.append(pltpu.make_async_copy(emb.at[rows], emb_v.at[rows], in_sem.at[h]))
        emb_in[h].start()
    ids_copy.start()

    barrier = pltpu.get_barrier_semaphore()

    def greet(where):
        pl.semaphore_signal(barrier, inc=1, device_id=where, device_id_type=MESH)

    greet(device(plane - 1, n_from, core))
    greet(device(plane, lax.rem(y + 1, 4) * 2 + x, core))
    greet(device(plane, lax.rem(y + 3, 4) * 2 + x, core))
    greet(device(plane, n_x, core))
    greet(device(plane, n, 1 - core))

    @pl.when(core == 1)
    def _():
        greet(device(plane, n_x, 0))

    def remote(src, dst, send, recv, where):
        return pltpu.make_async_remote_copy(
            src_ref=src,
            dst_ref=dst,
            send_sem=send,
            recv_sem=recv,
            device_id=where,
            device_id_type=MESH,
        )

    def piece(k):
        return pl.ds(HEAD + k * CH, CH) if k else pl.ds(0, HEAD + CH)

    def y_peer(d):
        return device(plane, lax.rem(y + d, 4) * 2 + x, core)

    def y_copy(d, k):
        slot = 2 if d == 1 else 1
        src, dst = r_unit.at[0, piece(k)], r_unit.at[slot, piece(k)]
        return remote(src, dst, y_send.at[slot - 1, k], r_recv.at[slot, k], y_peer(d))

    def relay_copy(slot, k):
        src, dst = r_unit.at[slot, piece(k)], r_unit.at[3, piece(k)]
        where = y_peer(3 if slot == 1 else 1)
        return remote(src, dst, relay_send.at[slot - 1, k % 2], r_recv.at[3, k], where)

    def p_copy(k):
        src, dst = r_unit.at[0, piece(k)], s_unit.at[p_slot, piece(k)]
        return remote(src, dst, p_send.at[k], s_recv.at[p_slot, k], device(plane + 1, n_p, core))

    def f_copy(k):
        src, dst = s_unit.at[p_slot, piece(k)], s_unit.at[f_slot, piece(k)]
        return remote(src, dst, f_send.at[k], s_recv.at[f_slot, k], device(plane, n_x, core))

    def q0_copy(i, k):
        src, dst = r_unit.at[0, piece(k)], s_unit.at[i, piece(k)]
        where = device(plane, n_x if i else n, 1)
        return remote(src, dst, q_send.at[i, k], s_recv.at[i, k], where)

    def q1_copy(i, k):
        src, dst = s_unit.at[2 + i, piece(k)], s_unit.at[1 + 2 * i, piece(k)]
        where = device(plane, n, 0)
        return remote(src, dst, q_send.at[i, k], s_recv.at[1 + 2 * i, k], where)

    ids_copy.wait()
    clusters = jnp.concatenate(
        [ids[...].astype(jnp.float32), jnp.zeros((HEAD - GROUPS, LANES), jnp.float32)], axis=0
    )
    r_unit[0, :HEAD, :LANES] = clusters.astype(jnp.bfloat16)
    r_unit[0, :HEAD, LANES:] = jnp.zeros((HEAD, SK - LANES), jnp.bfloat16)
    proj_in.wait()
    for h in range(2):
        emb_in[h].wait()
        rows = slice(h * HALF, (h + 1) * HALF)
        sketch = jnp.dot(emb_v[rows, :], proj_v[...], preferred_element_type=jnp.float32)
        squares = jnp.sum(sketch * sketch, axis=1, keepdims=True)
        unit = (sketch * lax.rsqrt(squares + 1e-06)).astype(jnp.bfloat16)
        r_unit[0, HEAD + h * HALF : HEAD + (h + 1) * HALF, :] = unit
        if h == 0:
            pl.semaphore_wait(barrier, 6 - core)
        near = (2 * h, 2 * h + 1)
        for k in near:
            p_copy(k).start()
            y_copy(1, k).start()
            if h == 1:
                y_copy(3, k).start()
        y_copy(3, h).start()

        @pl.when(core == 0)
        def _():
            for k in near:
                if k < 3:
                    q0_copy(1, k).start()
                    q0_copy(0, k).start()

    def clusters_of(unit, slot):
        return unit[slot, :HEAD, :LANES].astype(jnp.float32)

    def columns(slot):
        rows = clusters_of(r_unit, slot)
        for j in range(GROUPS):
            row = jnp.broadcast_to(rows[j : j + 1, :], (LANES, LANES))
            r_col[slot, j * LANES : (j + 1) * LANES, :] = row.T

    columns(0)
    row_acc[...] = jnp.full_like(row_acc, -1.0)

    def landed(ref, sem):
        pltpu.make_async_copy(ref, ref, sem).wait()

    def r_wait(d, k):
        landed(r_unit.at[d, piece(k)], r_recv.at[d, k])

    def s_wait(s, k):
        landed(s_unit.at[s, piece(k)], s_recv.at[s, k])

    def to_core_0(i, k):
        @pl.when(core == 1)
        def _():
            q1_copy(i, k).start()

    for k in range(CHUNKS):
        if k < 2:
            for slot, piece_of in ((1, 2 + k), (2, k)):
                r_wait(slot, piece_of)
                relay_copy(slot, piece_of).start()
        if k == 0:

            @pl.when(core == 0)
            def _():
                q0_copy(1, 3).start()
                q0_copy(0, 3).start()

        s_wait(p_slot, k)
        f_copy(k).start()
        to_core_0(0, k)

    s_wait(f_slot, 0)
    pl.semaphore_signal(ready, inc=1, device_id=device(plane + 1, n_p, core), device_id_type=MESH)
    to_core_0(1, 0)
    for k in range(2):
        r_wait(1, k)
        r_wait(2, 2 + k)
    columns(1)
    columns(2)
    for k in range(CHUNKS):
        r_wait(3, k)
    columns(3)

    def arrive(s):
        @pl.when(jnp.logical_and(s != p_slot, s != 4 - core))
        def _():
            @pl.when(s != f_slot)
            def _():
                s_wait(s, 0)

            for k in range(1, CHUNKS):
                s_wait(s, k)

        for k in range(1, CHUNKS):

            @pl.when(jnp.logical_and(core == 1, s == k))
            def _():
                s_wait(3, k)
                if k == 3:
                    pl.semaphore_wait(ready, 1)
                q1_copy(1, k).start()

    def score(r, s, s_clusters, peaks, best):
        scores = lax.dot_general(
            r_unit[r, HEAD:],
            s_unit[s, HEAD:],
            (((1,), (1,)), ((), ())),
            preferred_element_type=jnp.float32,
        )
        a_ids = r_col[r]
        for j in range(GROUPS):
            lanes = slice(j * LANES, (j + 1) * LANES)
            kept = jnp.where(a_ids == s_clusters[j : j + 1, :], scores[:, lanes], -1.0)
            best = jnp.maximum(best, kept)
            peaks[j] = jnp.maximum(peaks[j], jnp.max(kept.reshape(ROWS // 8, 8, LANES), axis=0))
        return best

    @pl.loop(0, 3)
    def _(s):
        arrive(s)
        s_clusters = clusters_of(s_unit, s)
        peaks = [jnp.full((8, LANES), -1.0, jnp.float32)] * GROUPS
        for r in range(4):
            row_acc[r] = score(r, s, s_clusters, peaks, row_acc[r])
        for j in range(GROUPS):
            col_acc[s, j] = peaks[j]

    arrive(jnp.int32(3))
    s_clusters = clusters_of(s_unit, 3)
    peaks = [jnp.full((8, LANES), -1.0, jnp.float32)] * GROUPS
    for r in range(4):
        best = score(r, 3, s_clusters, peaks, row_acc[r])
        at = lax.rem(y + (0, 1, 3, 2)[r], 4)
        for j in range(GROUPS):
            part = best[j * LANES : (j + 1) * LANES, :].T
            row_all[n, at, j : j + 1, :] = jnp.max(part, axis=0, keepdims=True)

    def tail(src, dst, kind, where):
        return remote(src, dst, tail_send.at[kind], tail_recv.at[kind], where)

    for k in range(1, 8):
        tail(row_all.at[n], row_all.at[n], 0, device(plane, lax.rem(n + k, 8), core)).start()

    for s in range(4):
        block = jnp.where(core == 0, s % 2, 1 - s // 2)
        x_0 = x_p if s < 2 else 1 - x_p
        x_1 = (x, 1 - x, x_p, 1 - x_p)[s]
        x_abs = jnp.where(core == 0, x_0, x_1)
        for j in range(GROUPS):
            peak = peaks[j] if s == 3 else col_acc[s, j]
            col_src[block, x_abs, j : j + 1, :] = jnp.max(peak, axis=0, keepdims=True)

    @pl.when(core == 0)
    def _():
        pl.semaphore_wait(ready, 1)

    for k in range(8):
        tail(col_src.at[0], col_all.at[0, n], 1, device(plane - 1, k, core)).start()
        tail(col_src.at[1], col_all.at[1, n], 1, device(plane - 1 + core, k, 1 - core)).start()

    some = row_all.at[pl.ds(0, 7)]
    landed(some, tail_recv.at[0])
    landed(col_all, tail_recv.at[1])
    for y_abs in range(4):
        for x_abs in range(2):
            best = jnp.full((GROUPS, LANES), -1.0, jnp.float32)
            for y_from in range(4):
                best = jnp.maximum(best, row_all[y_from * 2 + x_abs, y_abs])
            for g in range(2):
                for x_from in range(2):
                    best = jnp.maximum(best, col_all[g, y_abs * 2 + x_from, x_abs])
            out[y_abs * 2 + x_abs] = best

    landed(some, tail_send.at[0])
    landed(col_all, tail_send.at[1])
    for k in range(CHUNKS):
        y_copy(1, k).wait_send()
        y_copy(3, k).wait_send()
        relay_copy(1 if k >= 2 else 2, k).wait_send()
        p_copy(k).wait_send()
        f_copy(k).wait_send()
        for i in range(2):
            landed(r_unit.at[0, piece(k)], q_send.at[i, k])


def body(embeddings, projection, cluster_id):
    dma = pltpu.SemaphoreType.DMA
    operands = embeddings, projection, cluster_id.reshape(GROUPS, LANES)
    best = pl.pallas_call(
        kernel,
        out_shape=jax.ShapeDtypeStruct((8, GROUPS, LANES), jnp.float32),
        in_specs=[
            pl.BlockSpec(memory_space=pltpu.HBM),
            pl.BlockSpec(memory_space=pltpu.HBM),
            pl.BlockSpec(memory_space=pltpu.HBM),
        ],
        out_specs=pl.BlockSpec(memory_space=pltpu.VMEM),
        scratch_shapes=[
            pltpu.VMEM((ROWS, D), jnp.bfloat16),
            pltpu.VMEM((D, SK), jnp.bfloat16),
            pltpu.VMEM((GROUPS, LANES), jnp.int32),
            pltpu.VMEM((4, HEAD + ROWS, SK), jnp.bfloat16),
            pltpu.VMEM((4, HEAD + ROWS, SK), jnp.bfloat16),
            pltpu.VMEM((4, ROWS, LANES), jnp.float32),
            pltpu.VMEM((4, ROWS, LANES), jnp.float32),
            pltpu.VMEM((4, GROUPS, 8, LANES), jnp.float32),
            pltpu.VMEM((8, 4, GROUPS, LANES), jnp.float32),
            pltpu.VMEM((2, 2, GROUPS, LANES), jnp.float32),
            pltpu.VMEM((2, 8, 2, GROUPS, LANES), jnp.float32),
            dma((4,)),
            dma((2, CHUNKS)),
            dma((2, 2)),
            dma((4, CHUNKS)),
            dma((CHUNKS,)),
            dma((CHUNKS,)),
            dma((2, CHUNKS)),
            dma((4, CHUNKS)),
            dma((2,)),
            dma((2,)),
            pltpu.SemaphoreType.REGULAR,
        ],
        compiler_params=pltpu.CompilerParams(
            collective_id=0, has_side_effects=True, vmem_limit_bytes=32 << 20
        ),
        name="best_match",
    )(*(pltpu.with_memory_space_constraint(a, pltpu.HBM) for a in operands))
    return best.reshape(8 * ROWS)


def solution(mesh):
    in_specs = (P(("wide", "narrow"), None), P(), P(("wide", "narrow")))
    out_specs = P("wide")
    return jax.shard_map(body, mesh=mesh, in_specs=in_specs, out_specs=out_specs, check_vma=False)
```

```python
import jax
import jax.numpy as jnp
from jax import lax
from jax.experimental import pallas as pl
from jax.experimental.pallas import tpu as pltpu
from jax.sharding import PartitionSpec as P

MESH = pl.DeviceIdType.MESH
ROWS = 512
SK = 256
D = 1024
CHUNKS = 4
CH = ROWS // CHUNKS
HALF = ROWS // 2
HEAD = 16
PLANES = 16
LANES = 128
GROUPS = ROWS // LANES


def device(plane, n, core):
    return (lax.rem(plane + PLANES, PLANES) * 2 + core, n)


def kernel(
    emb,
    proj,
    ids_in,
    out,
    emb_v,
    proj_v,
    ids,
    r_unit,
    s_unit,
    r_col,
    row_acc,
    col_acc,
    row_all,
    col_src,
    col_all,
    in_sem,
    y_send,
    relay_send,
    r_recv,
    p_send,
    f_send,
    d_send,
    q_send,
    s_recv,
    tail_send,
    tail_recv,
    ready,
):
    wide, n = lax.axis_index("wide"), lax.axis_index("narrow")
    plane, core = wide // 2, lax.rem(wide, 2)
    y, x = n // 2, lax.rem(n, 2)
    n_x = y * 2 + 1 - x
    crosses_out = lax.rem(plane, 8) == 7
    crosses_in = lax.rem(plane, 8) == 0
    n_p = jnp.where(crosses_out, n_x, n)
    n_f = jnp.where(crosses_out, n, n_x)
    x_p = jnp.where(crosses_in, 1 - x, x)
    p_slot, f_slot = 2 * core, 2 + core

    def load(src, dst, size, i, sem):
        rows = pl.ds(i * size, size)
        return pltpu.make_async_copy(src.at[rows], dst.at[rows], in_sem.at[sem])

    ids_copy = pltpu.make_async_copy(ids_in, ids, in_sem.at[0])
    emb_in = [load(emb, emb_v, CH, k, 1 + k) for k in range(4)]
    proj_in = [load(proj, proj_v, D // 4, k, 5 + k) for k in range(4)]
    for copy in (ids_copy, *proj_in, *emb_in):
        copy.start()

    barrier = pltpu.get_barrier_semaphore()

    def greet(where):
        pl.semaphore_signal(barrier, inc=1, device_id=where, device_id_type=MESH)

    greet(device(plane - 1, n, core))
    greet(device(plane - 1, n_x, core))
    greet(device(plane, lax.rem(y + 1, 4) * 2 + x, core))
    greet(device(plane, lax.rem(y + 3, 4) * 2 + x, core))
    greet(device(plane, n_x, core))
    greet(device(plane, n, 1 - core))

    @pl.when(core == 1)
    def _():
        greet(device(plane, n_x, 0))

    def remote(src, dst, send, recv, where):
        return pltpu.make_async_remote_copy(
            src_ref=src,
            dst_ref=dst,
            send_sem=send,
            recv_sem=recv,
            device_id=where,
            device_id_type=MESH,
        )

    def piece(k):
        return pl.ds(HEAD + k * CH, CH) if k else pl.ds(0, HEAD + CH)

    def y_peer(d):
        return device(plane, lax.rem(y + d, 4) * 2 + x, core)

    def y_copy(d, k):
        slot = 2 if d == 1 else 1
        src, dst = r_unit.at[0, piece(k)], r_unit.at[slot, piece(k)]
        return remote(src, dst, y_send.at[slot - 1, k], r_recv.at[slot, k], y_peer(d))

    def relay_copy(slot, k):
        src, dst = r_unit.at[slot, piece(k)], r_unit.at[3, piece(k)]
        where = y_peer(3 if slot == 1 else 1)
        return remote(src, dst, relay_send.at[slot - 1, k % 2], r_recv.at[3, k], where)

    def p_copy(k):
        src, dst = r_unit.at[0, piece(k)], s_unit.at[p_slot, piece(k)]
        return remote(src, dst, p_send.at[k], s_recv.at[p_slot, k], device(plane + 1, n_p, core))

    def f_copy(k):
        src, dst = s_unit.at[p_slot, piece(k)], s_unit.at[f_slot, piece(k)]
        return remote(src, dst, f_send.at[k], s_recv.at[f_slot, k], device(plane, n_x, core))

    def d_copy():
        src, dst = r_unit.at[0, piece(3)], s_unit.at[f_slot, piece(3)]
        where = device(plane + 1, n_f, core)
        return remote(src, dst, d_send.at[0], s_recv.at[f_slot, 3], where)

    def q0_copy(i, k):
        src, dst = r_unit.at[0, piece(k)], s_unit.at[i, piece(k)]
        where = device(plane, n_x if i else n, 1)
        return remote(src, dst, q_send.at[i, k], s_recv.at[i, k], where)

    def q1_copy(i, k):
        src, dst = s_unit.at[2 + i, piece(k)], s_unit.at[1 + 2 * i, piece(k)]
        where = device(plane, n, 0)
        return remote(src, dst, q_send.at[i, k], s_recv.at[1 + 2 * i, k], where)

    ids_copy.wait()
    clusters = jnp.concatenate(
        [ids[...].astype(jnp.float32), jnp.zeros((HEAD - GROUPS, LANES), jnp.float32)], axis=0
    )
    r_unit[0, :HEAD, :LANES] = clusters.astype(jnp.bfloat16)
    r_unit[0, :HEAD, LANES:] = jnp.zeros((HEAD, SK - LANES), jnp.bfloat16)
    for copy in proj_in:
        copy.wait()
    for h in range(2):
        emb_in[2 * h].wait()
        emb_in[2 * h + 1].wait()
        rows = slice(h * HALF, (h + 1) * HALF)
        sketch = jnp.dot(emb_v[rows, :], proj_v[...], preferred_element_type=jnp.float32)
        squares = jnp.sum(sketch * sketch, axis=1, keepdims=True)
        unit = (sketch * lax.rsqrt(squares + 1e-06)).astype(jnp.bfloat16)
        r_unit[0, HEAD + h * HALF : HEAD + (h + 1) * HALF, :] = unit
        if h == 0:
            pl.semaphore_wait(barrier, 7 - core)
        near = (2 * h, 2 * h + 1)
        for k in near:
            if k == 3:
                d_copy().start()
            p_copy(k).start()
            y_copy(1, k).start()
            if h == 1:
                y_copy(3, k).start()
        y_copy(3, h).start()

        @pl.when(core == 0)
        def _():
            for k in near:
                if k < 3:
                    q0_copy(1, k).start()
                    q0_copy(0, k).start()

    def clusters_of(unit, slot):
        return unit[slot, :HEAD, :LANES].astype(jnp.float32)

    def columns(slot):
        rows = clusters_of(r_unit, slot)
        for j in range(GROUPS):
            row = jnp.broadcast_to(rows[j : j + 1, :], (LANES, LANES))
            r_col[slot, j * LANES : (j + 1) * LANES, :] = row.T

    columns(0)
    row_acc[...] = jnp.full_like(row_acc, -1.0)

    def landed(ref, sem):
        pltpu.make_async_copy(ref, ref, sem).wait()

    def r_wait(d, k):
        landed(r_unit.at[d, piece(k)], r_recv.at[d, k])

    def s_wait(s, k):
        landed(s_unit.at[s, piece(k)], s_recv.at[s, k])

    def to_core_0(i, k):
        @pl.when(core == 1)
        def _():
            q1_copy(i, k).start()

    for k in range(CHUNKS):
        if k < 2:
            for slot, piece_of in ((1, 2 + k), (2, k)):
                r_wait(slot, piece_of)
                relay_copy(slot, piece_of).start()
        if k == 0:

            @pl.when(core == 0)
            def _():
                q0_copy(1, 3).start()
                q0_copy(0, 3).start()

        s_wait(p_slot, k)
        if k < 3:
            f_copy(k).start()
        to_core_0(0, k)

    s_wait(f_slot, 0)
    pl.semaphore_signal(ready, inc=1, device_id=device(plane + 1, n_p, core), device_id_type=MESH)
    to_core_0(1, 0)
    for k in range(2):
        r_wait(1, k)
        r_wait(2, 2 + k)
    columns(1)
    columns(2)
    for k in range(CHUNKS):
        r_wait(3, k)
    columns(3)

    def arrive(s):
        @pl.when(jnp.logical_and(s != p_slot, s != 4 - core))
        def _():
            @pl.when(s != f_slot)
            def _():
                s_wait(s, 0)

            for k in range(1, CHUNKS):
                s_wait(s, k)

        for k in range(1, CHUNKS):

            @pl.when(jnp.logical_and(core == 1, s == k))
            def _():
                s_wait(3, k)
                if k == 3:
                    pl.semaphore_wait(ready, 1)
                q1_copy(1, k).start()

    def score(r, s, s_clusters, peaks, best):
        scores = lax.dot_general(
            r_unit[r, HEAD:],
            s_unit[s, HEAD:],
            (((1,), (1,)), ((), ())),
            preferred_element_type=jnp.float32,
        )
        a_ids = r_col[r]
        for j in range(GROUPS):
            lanes = slice(j * LANES, (j + 1) * LANES)
            kept = jnp.where(a_ids == s_clusters[j : j + 1, :], scores[:, lanes], -1.0)
            best = jnp.maximum(best, kept)
            peaks[j] = jnp.maximum(peaks[j], jnp.max(kept.reshape(ROWS // 8, 8, LANES), axis=0))
        return best

    @pl.loop(0, 3)
    def _(s):
        arrive(s)
        s_clusters = clusters_of(s_unit, s)
        peaks = [jnp.full((8, LANES), -1.0, jnp.float32)] * GROUPS
        for r in range(4):
            row_acc[r] = score(r, s, s_clusters, peaks, row_acc[r])
        for j in range(GROUPS):
            col_acc[s, j] = peaks[j]

    arrive(jnp.int32(3))
    s_clusters = clusters_of(s_unit, 3)
    peaks = [jnp.full((8, LANES), -1.0, jnp.float32)] * GROUPS
    for r in range(4):
        best = score(r, 3, s_clusters, peaks, row_acc[r])
        at = lax.rem(y + (0, 1, 3, 2)[r], 4)
        for j in range(GROUPS):
            part = best[j * LANES : (j + 1) * LANES, :].T
            row_all[n, at, j : j + 1, :] = jnp.max(part, axis=0, keepdims=True)

    def tail(src, dst, kind, where):
        return remote(src, dst, tail_send.at[kind], tail_recv.at[kind], where)

    for k in range(1, 8):
        tail(row_all.at[n], row_all.at[n], 0, device(plane, lax.rem(n + k, 8), core)).start()

    for s in range(4):
        block = jnp.where(core == 0, s % 2, 1 - s // 2)
        x_0 = x_p if s < 2 else 1 - x_p
        x_1 = (x, 1 - x, x_p, 1 - x_p)[s]
        x_abs = jnp.where(core == 0, x_0, x_1)
        for j in range(GROUPS):
            peak = peaks[j] if s == 3 else col_acc[s, j]
            col_src[block, x_abs, j : j + 1, :] = jnp.max(peak, axis=0, keepdims=True)

    @pl.when(core == 0)
    def _():
        pl.semaphore_wait(ready, 1)

    for k in range(8):
        tail(col_src.at[0], col_all.at[0, n], 1, device(plane - 1, k, core)).start()
        tail(col_src.at[1], col_all.at[1, n], 1, device(plane - 1 + core, k, 1 - core)).start()

    some = row_all.at[pl.ds(0, 7)]
    landed(some, tail_recv.at[0])
    landed(col_all, tail_recv.at[1])
    for y_abs in range(4):
        for x_abs in range(2):
            best = jnp.full((GROUPS, LANES), -1.0, jnp.float32)
            for y_from in range(4):
                best = jnp.maximum(best, row_all[y_from * 2 + x_abs, y_abs])
            for g in range(2):
                for x_from in range(2):
                    best = jnp.maximum(best, col_all[g, y_abs * 2 + x_from, x_abs])
            out[y_abs * 2 + x_abs] = best

    landed(some, tail_send.at[0])
    landed(col_all, tail_send.at[1])
    for k in range(CHUNKS):
        y_copy(1, k).wait_send()
        y_copy(3, k).wait_send()
        relay_copy(1 if k >= 2 else 2, k).wait_send()
        p_copy(k).wait_send()
        if k < 3:
            f_copy(k).wait_send()
        else:
            d_copy().wait_send()
        for i in range(2):
            landed(r_unit.at[0, piece(k)], q_send.at[i, k])


def body(embeddings, projection, cluster_id):
    dma = pltpu.SemaphoreType.DMA
    operands = embeddings, projection, cluster_id.reshape(GROUPS, LANES)
    best = pl.pallas_call(
        kernel,
        out_shape=jax.ShapeDtypeStruct((8, GROUPS, LANES), jnp.float32),
        in_specs=[
            pl.BlockSpec(memory_space=pltpu.HBM),
            pl.BlockSpec(memory_space=pltpu.HBM),
            pl.BlockSpec(memory_space=pltpu.HBM),
        ],
        out_specs=pl.BlockSpec(memory_space=pltpu.VMEM),
        scratch_shapes=[
            pltpu.VMEM((ROWS, D), jnp.bfloat16),
            pltpu.VMEM((D, SK), jnp.bfloat16),
            pltpu.VMEM((GROUPS, LANES), jnp.int32),
            pltpu.VMEM((4, HEAD + ROWS, SK), jnp.bfloat16),
            pltpu.VMEM((4, HEAD + ROWS, SK), jnp.bfloat16),
            pltpu.VMEM((4, ROWS, LANES), jnp.float32),
            pltpu.VMEM((4, ROWS, LANES), jnp.float32),
            pltpu.VMEM((4, GROUPS, 8, LANES), jnp.float32),
            pltpu.VMEM((8, 4, GROUPS, LANES), jnp.float32),
            pltpu.VMEM((2, 2, GROUPS, LANES), jnp.float32),
            pltpu.VMEM((2, 8, 2, GROUPS, LANES), jnp.float32),
            dma((9,)),
            dma((2, CHUNKS)),
            dma((2, 2)),
            dma((4, CHUNKS)),
            dma((CHUNKS,)),
            dma((CHUNKS - 1,)),
            dma((1,)),
            dma((2, CHUNKS)),
            dma((4, CHUNKS)),
            dma((2,)),
            dma((2,)),
            pltpu.SemaphoreType.REGULAR,
        ],
        compiler_params=pltpu.CompilerParams(
            collective_id=0, has_side_effects=True, vmem_limit_bytes=32 << 20
        ),
        name="best_match",
    )(*(pltpu.with_memory_space_constraint(a, pltpu.HBM) for a in operands))
    return best.reshape(8 * ROWS)


def solution(mesh):
    in_specs = (P(("wide", "narrow"), None), P(), P(("wide", "narrow")))
    out_specs = P("wide")
    return jax.shard_map(body, mesh=mesh, in_specs=in_specs, out_specs=out_specs, check_vma=False)
```

```python
import jax
import jax.numpy as jnp
from jax import lax
from jax.experimental import pallas as pl
from jax.experimental.pallas import tpu as pltpu
from jax.sharding import PartitionSpec as P

MESH = pl.DeviceIdType.MESH
ROWS = 512
SK = 256
D = 1024
CHUNKS = 4
CH = ROWS // CHUNKS
HEAD = 16
UP = ((0, 144), (144, 128), (272, 64), (336, 64), (400, 128))
LAST = len(UP) - 1
PLANES = 16
LANES = 128
GROUPS = ROWS // LANES


def device(plane, n, core):
    return (lax.rem(plane + PLANES, PLANES) * 2 + core, n)


def kernel(
    emb,
    proj,
    ids_in,
    out,
    emb_v,
    proj_v,
    ids,
    r_unit,
    s_unit,
    r_col,
    row_acc,
    col_acc,
    row_all,
    col_src,
    col_all,
    in_sem,
    y_send,
    relay_send,
    r_recv,
    p_send,
    f_send,
    q_send,
    s_recv,
    tail_send,
    tail_recv,
    ready,
):
    wide, n = lax.axis_index("wide"), lax.axis_index("narrow")
    plane, core = wide // 2, lax.rem(wide, 2)
    y, x = n // 2, lax.rem(n, 2)
    n_x = y * 2 + 1 - x
    crosses_out = lax.rem(plane, 8) == 7
    crosses_in = lax.rem(plane, 8) == 0
    n_p = jnp.where(crosses_out, n_x, n)
    n_f = jnp.where(crosses_out, n, n_x)
    x_p = jnp.where(crosses_in, 1 - x, x)
    p_slot, f_slot = 2 * core, 2 + core

    first, rest = pl.ds(0, CH), pl.ds(CH, ROWS - CH)
    loads = [
        pltpu.make_async_copy(proj, proj_v, in_sem.at[0]),
        pltpu.make_async_copy(emb.at[first], emb_v.at[first], in_sem.at[1]),
        pltpu.make_async_copy(ids_in, ids, in_sem.at[2]),
        pltpu.make_async_copy(emb.at[rest], emb_v.at[rest], in_sem.at[3]),
    ]
    for copy in loads:
        copy.start()

    barrier = pltpu.get_barrier_semaphore()

    def greet(where):
        pl.semaphore_signal(barrier, inc=1, device_id=where, device_id_type=MESH)

    greet(device(plane - 1, n, core))
    greet(device(plane - 1, n_x, core))
    greet(device(plane, lax.rem(y + 1, 4) * 2 + x, core))
    greet(device(plane, lax.rem(y + 3, 4) * 2 + x, core))
    greet(device(plane, n_x, core))
    greet(device(plane, n, 1 - core))

    @pl.when(core == 1)
    def _():
        greet(device(plane, n_x, 0))

    def remote(src, dst, send, recv, where):
        return pltpu.make_async_remote_copy(
            src_ref=src,
            dst_ref=dst,
            send_sem=send,
            recv_sem=recv,
            device_id=where,
            device_id_type=MESH,
        )

    def piece(k):
        return pl.ds(HEAD + k * CH, CH) if k else pl.ds(0, HEAD + CH)

    def y_peer(d):
        return device(plane, lax.rem(y + d, 4) * 2 + x, core)

    def y_copy(d, k):
        slot = 2 if d == 1 else 1
        src, dst = r_unit.at[0, piece(k)], r_unit.at[slot, piece(k)]
        return remote(src, dst, y_send.at[slot - 1, k], r_recv.at[slot, k], y_peer(d))

    def relay_copy(slot, k):
        src, dst = r_unit.at[slot, piece(k)], r_unit.at[3, piece(k)]
        where = y_peer(3 if slot == 1 else 1)
        return remote(src, dst, relay_send.at[slot - 1, k % 2], r_recv.at[3, k], where)

    def up(k):
        return pl.ds(*UP[k])

    def p_copy(k):
        src, dst = r_unit.at[0, up(k)], s_unit.at[p_slot, up(k)]
        return remote(src, dst, p_send.at[k], s_recv.at[p_slot, k], device(plane + 1, n_p, core))

    def f_copy(k):
        here = s_unit.at[p_slot, up(k)] if k < LAST else r_unit.at[0, up(k)]
        where = device(plane, n_x, core) if k < LAST else device(plane + 1, n_f, core)
        return remote(here, s_unit.at[f_slot, up(k)], f_send.at[k], s_recv.at[f_slot, k], where)

    def q0_rows(k):
        return up(k) if k == LAST else pl.ds(0, UP[LAST][0])

    def q0_copy(i, k):
        src, dst = r_unit.at[0, q0_rows(k)], s_unit.at[i, q0_rows(k)]
        where = device(plane, n_x if i else n, 1)
        return remote(src, dst, q_send.at[i, k], s_recv.at[i, k], where)

    def q1_copy(i, k):
        src, dst = s_unit.at[2 + i, up(k)], s_unit.at[1 + 2 * i, up(k)]
        where = device(plane, n, 0)
        return remote(src, dst, q_send.at[i, k], s_recv.at[1 + 2 * i, k], where)

    loads[2].wait()
    clusters = jnp.concatenate(
        [ids[...].astype(jnp.float32), jnp.zeros((HEAD - GROUPS, LANES), jnp.float32)], axis=0
    )
    r_unit[0, :HEAD, :LANES] = clusters.astype(jnp.bfloat16)
    r_unit[0, :HEAD, LANES:] = jnp.zeros((HEAD, SK - LANES), jnp.bfloat16)

    def make_units(start, stop):
        sketch = jnp.dot(emb_v[start:stop, :], proj_v[...], preferred_element_type=jnp.float32)
        squares = jnp.sum(sketch * sketch, axis=1, keepdims=True)
        unit = (sketch * lax.rsqrt(squares + 1e-06)).astype(jnp.bfloat16)
        r_unit[0, HEAD + start : HEAD + stop, :] = unit

    loads[0].wait()
    loads[1].wait()
    make_units(0, CH)
    pl.semaphore_wait(barrier, 7 - core)
    p_copy(0).start()
    y_copy(1, 0).start()
    y_copy(3, 0).start()
    loads[3].wait()
    make_units(CH, ROWS)
    p_copy(1).start()
    y_copy(1, 1).start()
    y_copy(3, 2).start()
    p_copy(2).start()
    p_copy(3).start()
    y_copy(1, 2).start()
    y_copy(3, 3).start()
    p_copy(LAST).start()
    f_copy(LAST).start()
    y_copy(1, 3).start()
    y_copy(3, 1).start()

    @pl.when(core == 0)
    def _():
        q0_copy(1, 0).start()
        q0_copy(0, 0).start()

    def clusters_of(unit, slot):
        return unit[slot, :HEAD, :LANES].astype(jnp.float32)

    def columns(slot):
        rows = clusters_of(r_unit, slot)
        for j in range(GROUPS):
            row = jnp.broadcast_to(rows[j : j + 1, :], (LANES, LANES))
            r_col[slot, j * LANES : (j + 1) * LANES, :] = row.T

    columns(0)
    row_acc[...] = jnp.full_like(row_acc, -1.0)

    def landed(ref, sem):
        pltpu.make_async_copy(ref, ref, sem).wait()

    def r_wait(d, k):
        landed(r_unit.at[d, piece(k)], r_recv.at[d, k])

    def s_wait(s, k):
        landed(s_unit.at[s, up(k)], s_recv.at[s, k])

    def to_core_0(i, k):
        @pl.when(core == 1)
        def _():
            q1_copy(i, k).start()

    def hand_on(pieces):
        for k in pieces:
            s_wait(3, k)
            q1_copy(1, k).start()

    def score(r, s, s_clusters, peaks, best):
        scores = lax.dot_general(
            r_unit[r, HEAD:],
            s_unit[s, HEAD:],
            (((1,), (1,)), ((), ())),
            preferred_element_type=jnp.float32,
        )
        a_ids = r_col[r]
        for j in range(GROUPS):
            lanes = slice(j * LANES, (j + 1) * LANES)
            kept = jnp.where(a_ids == s_clusters[j : j + 1, :], scores[:, lanes], -1.0)
            best = jnp.maximum(best, kept)
            peaks[j] = jnp.maximum(peaks[j], jnp.max(kept.reshape(ROWS // 8, 8, LANES), axis=0))
        return best

    def rows_done(r, best):
        at = lax.rem(y + (0, 1, 3, 2)[r], 4)
        for j in range(GROUPS):
            part = best[j * LANES : (j + 1) * LANES, :].T
            row_all[n, at, j : j + 1, :] = jnp.max(part, axis=0, keepdims=True)

    def score_half(r, s, half, s_clusters, peaks, best):
        keys = pl.ds(pl.multiple_of(HEAD + half * (ROWS // 2), HEAD), ROWS // 2)
        scores = lax.dot_general(
            r_unit[r, HEAD:],
            s_unit[s, keys, :],
            (((1,), (1,)), ((), ())),
            preferred_element_type=jnp.float32,
        )
        a_ids = r_col[r]
        for j in range(GROUPS // 2):
            b_ids = jnp.where(half == 0, s_clusters[j : j + 1, :], s_clusters[j + 2 : j + 3, :])
            kept = jnp.where(a_ids == b_ids, scores[:, j * LANES : (j + 1) * LANES], -1.0)
            best = jnp.maximum(best, kept)
            peaks[j] = jnp.maximum(peaks[j], jnp.max(kept.reshape(ROWS // 8, 8, LANES), axis=0))
        return best

    def half_slot(s, half, done):
        s_clusters = clusters_of(s_unit, s)
        peaks = empty()[: GROUPS // 2]
        for r in range(4):
            done(r, score_half(r, s, half, s_clusters, peaks, row_acc[r]))
        for j in range(GROUPS // 2):
            col_acc[s, half * 2 + j] = peaks[j]

    def keep(r, best):
        row_acc[r] = best

    def score_near(s, peaks):
        s_clusters = clusters_of(s_unit, s)
        for r in range(3):
            row_acc[r] = score(r, s, s_clusters, peaks, row_acc[r])

    def empty():
        return [jnp.full((8, LANES), -1.0, jnp.float32)] * GROUPS

    def up_and_over(pieces):
        for k in pieces:
            s_wait(p_slot, k)
            f_copy(k).start()
            to_core_0(0, k)

    def say_ready():
        s_wait(f_slot, 0)
        pl.semaphore_signal(ready, inc=1, device_id=device(plane + 1, n_p, core), device_id_type=MESH)
        to_core_0(1, 0)

    def on_core(which, pieces, act):
        @pl.when(core == which)
        def _():
            for k in pieces:
                act(k)

    def relay(k):
        for slot, piece_of in ((2, k), (1, 2 + k)):
            r_wait(slot, piece_of)
            relay_copy(slot, piece_of).start()

    def late_q0():
        for i in (1, 0):
            q0_copy(i, LAST).start()

    def r_wait_near():
        for k in range(2):
            r_wait(1, k)
            r_wait(2, 2 + k)
        columns(1)
        columns(2)

    def r_wait_far():
        for k in range(CHUNKS):
            r_wait(3, k)
        columns(3)

    def q0_wait(s):
        for k in (0, LAST):
            landed(s_unit.at[s, q0_rows(k)], s_recv.at[s, k])

    @pl.when(crosses_in)
    def _():
        relay(0)
        on_core(0, (0,), lambda _: late_q0())
        relay(1)

        @pl.loop(0, 7)
        def _(i):
            @pl.when(i == 0)
            def _():
                up_and_over((0, 1))
                r_wait_near()
                r_wait_far()
                on_core(1, (0, 1), q0_wait)

            @pl.when(i == 1)
            def _():
                up_and_over((2, 3))
                on_core(0, (0, 1), lambda k: s_wait(1, k))

            @pl.when(i == 2)
            def _():
                say_ready()
                on_core(0, (LAST,), lambda k: s_wait(0, k))

            @pl.when(i == 3)
            def _():
                on_core(0, (2, 3, LAST), lambda k: s_wait(1, k))
                on_core(1, (LAST,), lambda k: s_wait(2, k))
                to_core_0(0, LAST)

            @pl.when(i == 4)
            def _():
                on_core(0, (1,), lambda k: s_wait(2, k))

            @pl.when(i == 5)
            def _():
                on_core(0, (0, 1), lambda k: s_wait(3, k))
                on_core(1, (0,), lambda _: hand_on((1, 2)))

            @pl.when(i == 6)
            def _():
                on_core(0, (2, 3, LAST), lambda k: s_wait(2, k))
                on_core(1, (0,), lambda _: hand_on((3,)))
                on_core(1, (0,), lambda _: pl.semaphore_wait(ready, 1))
                on_core(1, (0,), lambda _: hand_on((LAST,)))

            s = jnp.where(core == 0, 2 * (i // 4) + lax.rem(i, 2), i // 2)
            half = jnp.where(core == 0, lax.rem(i, 4) // 2, lax.rem(i, 2))
            half_slot(s, half, keep)

        on_core(0, (2, 3, LAST), lambda k: s_wait(3, k))
        half_slot(3, 1, rows_done)

    @pl.when(jnp.logical_not(crosses_in))
    def _():
        relay(0)
        up_and_over((0,))
        on_core(0, (0,), lambda _: late_q0())
        up_and_over((1,))
        relay(1)
        up_and_over((2, 3))
        say_ready()
        s_wait(p_slot, LAST)
        to_core_0(0, LAST)
        r_wait_near()

        @pl.loop(0, 2)
        def _(s):
            @pl.when(jnp.logical_and(core == 0, s == 1))
            def _():
                for k in range(LAST + 1):
                    s_wait(1, k)

            @pl.when(core == 1)
            def _():
                q0_wait(s)

            peaks = empty()
            score_near(s, peaks)
            for j in range(GROUPS):
                col_acc[s, j] = peaks[j]

        @pl.when(core == 1)
        def _():
            hand_on((1, 2))

        r_wait_far()
        best = row_acc[3]
        for s in range(2):
            peaks = [col_acc[s, j] for j in range(GROUPS)]
            best = score(3, s, clusters_of(s_unit, s), peaks, best)
            for j in range(GROUPS):
                col_acc[s, j] = peaks[j]
        row_acc[3] = best

        @pl.when(core == 0)
        def _():
            for k in range(1, LAST + 1):
                s_wait(2, k)

        @pl.when(core == 1)
        def _():
            hand_on((3,))
            pl.semaphore_wait(ready, 1)
            hand_on((LAST,))

        peaks = empty()
        score_near(2, peaks)
        row_acc[3] = score(3, 2, clusters_of(s_unit, 2), peaks, row_acc[3])
        for j in range(GROUPS):
            col_acc[2, j] = peaks[j]

        @pl.when(core == 0)
        def _():
            for k in range(LAST + 1):
                s_wait(3, k)

        s_clusters = clusters_of(s_unit, 3)
        peaks = empty()
        for r in range(4):
            rows_done(r, score(r, 3, s_clusters, peaks, row_acc[r]))
        for j in range(GROUPS):
            col_acc[3, j] = peaks[j]

    def tail(src, dst, kind, where):
        return remote(src, dst, tail_send.at[kind], tail_recv.at[kind], where)

    def send_rows():
        for m in (
            *(device(plane, lax.rem(y + d, 4) * 2 + 1 - x, core) for d in (2, 1, 3)),
            *(y_peer(d) for d in (2, 1, 3)),
            device(plane, n_x, core),
        ):
            tail(row_all.at[n], row_all.at[n], 0, m).start()

    @pl.when(crosses_in)
    def _():
        send_rows()

    for s in range(4):
        block = jnp.where(core == 0, s % 2, 1 - s // 2)
        x_0 = x_p if s < 2 else 1 - x_p
        x_1 = (x, 1 - x, x_p, 1 - x_p)[s]
        x_abs = jnp.where(core == 0, x_0, x_1)
        for j in range(GROUPS):
            peak = jnp.max(col_acc[s, j], axis=0, keepdims=True)
            col_src[block, x_abs, j : j + 1, :] = peak

    @pl.when(core == 0)
    def _():
        pl.semaphore_wait(ready, 1)

    for k in range(8):
        tail(col_src.at[0], col_all.at[0, n], 1, device(plane - 1, k, core)).start()
        tail(col_src.at[1], col_all.at[1, n], 1, device(plane - 1 + core, k, 1 - core)).start()

    @pl.when(jnp.logical_not(crosses_in))
    def _():
        send_rows()

    for k in range(CHUNKS):
        y_copy(1, k).wait_send()
        y_copy(3, k).wait_send()
        relay_copy(1 if k >= 2 else 2, k).wait_send()
    for k in range(LAST + 1):
        p_copy(k).wait_send()
        f_copy(k).wait_send()
    for i in range(2):

        @pl.when(core == 0)
        def _():
            q0_copy(i, 0).wait_send()
            q0_copy(i, LAST).wait_send()

        @pl.when(core == 1)
        def _():
            for k in range(LAST + 1):
                q1_copy(i, k).wait_send()

    some = row_all.at[pl.ds(0, 7)]
    landed(some, tail_recv.at[0])
    landed(col_all, tail_recv.at[1])
    for y_abs in range(4):
        for x_abs in range(2):
            best = jnp.full((GROUPS, LANES), -1.0, jnp.float32)
            for y_from in range(4):
                best = jnp.maximum(best, row_all[y_from * 2 + x_abs, y_abs])
            for g in range(2):
                for x_from in range(2):
                    best = jnp.maximum(best, col_all[g, y_abs * 2 + x_from, x_abs])
            out[y_abs * 2 + x_abs] = best

    landed(some, tail_send.at[0])
    landed(col_all, tail_send.at[1])


def body(embeddings, projection, cluster_id):
    dma = pltpu.SemaphoreType.DMA
    operands = embeddings, projection, cluster_id.reshape(GROUPS, LANES)
    best = pl.pallas_call(
        kernel,
        out_shape=jax.ShapeDtypeStruct((8, GROUPS, LANES), jnp.float32),
        in_specs=[
            pl.BlockSpec(memory_space=pltpu.HBM),
            pl.BlockSpec(memory_space=pltpu.HBM),
            pl.BlockSpec(memory_space=pltpu.HBM),
        ],
        out_specs=pl.BlockSpec(memory_space=pltpu.VMEM),
        scratch_shapes=[
            pltpu.VMEM((ROWS, D), jnp.bfloat16),
            pltpu.VMEM((D, SK), jnp.bfloat16),
            pltpu.VMEM((GROUPS, LANES), jnp.int32),
            pltpu.VMEM((4, HEAD + ROWS, SK), jnp.bfloat16),
            pltpu.VMEM((4, HEAD + ROWS, SK), jnp.bfloat16),
            pltpu.VMEM((4, ROWS, LANES), jnp.float32),
            pltpu.VMEM((4, ROWS, LANES), jnp.float32),
            pltpu.VMEM((4, GROUPS, 8, LANES), jnp.float32),
            pltpu.VMEM((8, 4, GROUPS, LANES), jnp.float32),
            pltpu.VMEM((2, 2, GROUPS, LANES), jnp.float32),
            pltpu.VMEM((2, 8, 2, GROUPS, LANES), jnp.float32),
            dma((4,)),
            dma((2, CHUNKS)),
            dma((2, 2)),
            dma((4, CHUNKS)),
            dma((LAST + 1,)),
            dma((LAST + 1,)),
            dma((2, LAST + 1)),
            dma((4, LAST + 1)),
            dma((2,)),
            dma((2,)),
            pltpu.SemaphoreType.REGULAR,
        ],
        compiler_params=pltpu.CompilerParams(
            collective_id=0, has_side_effects=True, vmem_limit_bytes=32 << 20
        ),
        name="best_match",
    )(*(pltpu.with_memory_space_constraint(a, pltpu.HBM) for a in operands))
    return best.reshape(8 * ROWS)


def solution(mesh):
    in_specs = (P(("wide", "narrow"), None), P(), P(("wide", "narrow")))
    out_specs = P("wide")
    return jax.shard_map(body, mesh=mesh, in_specs=in_specs, out_specs=out_specs, check_vma=False)
```

```python
import jax
import jax.numpy as jnp
from jax import lax
from jax.experimental import pallas as pl
from jax.experimental.pallas import tpu as pltpu
from jax.sharding import PartitionSpec as P

MESH = pl.DeviceIdType.MESH
ROWS = 512
SK = 256
D = 1024
CHUNKS = 4
CH = ROWS // CHUNKS
HEAD = 16
UP = ((0, 144), (144, 128), (272, 96), (368, 64), (432, 96))
LAST = len(UP) - 1
PLANES = 16
LANES = 128
GROUPS = ROWS // LANES


def device(plane, n, core):
    return (lax.rem(plane + PLANES, PLANES) * 2 + core, n)


def kernel(
    emb,
    proj,
    ids_in,
    out,
    emb_v,
    proj_v,
    ids,
    r_unit,
    s_unit,
    r_col,
    row_acc,
    col_acc,
    row_all,
    col_src,
    col_all,
    in_sem,
    y_send,
    relay_send,
    r_recv,
    p_send,
    f_send,
    q_send,
    s_recv,
    tail_send,
    tail_recv,
    ready,
    seen,
):
    wide, n = lax.axis_index("wide"), lax.axis_index("narrow")
    plane, core = wide // 2, lax.rem(wide, 2)
    y, x = n // 2, lax.rem(n, 2)
    n_x = y * 2 + 1 - x
    crosses_out = lax.rem(plane, 8) == 7
    crosses_in = lax.rem(plane, 8) == 0
    n_p = jnp.where(crosses_out, n_x, n)
    n_f = jnp.where(crosses_out, n, n_x)
    x_p = jnp.where(crosses_in, 1 - x, x)
    p_slot, f_slot = 2 * core, 2 + core

    first, rest = pl.ds(0, CH), pl.ds(CH, ROWS - CH)
    loads = [
        pltpu.make_async_copy(proj, proj_v, in_sem.at[0]),
        pltpu.make_async_copy(emb.at[first], emb_v.at[first], in_sem.at[1]),
        pltpu.make_async_copy(ids_in, ids, in_sem.at[2]),
        pltpu.make_async_copy(emb.at[rest], emb_v.at[rest], in_sem.at[3]),
    ]
    for copy in loads:
        copy.start()

    barrier = pltpu.get_barrier_semaphore()

    def greet(where):
        pl.semaphore_signal(barrier, inc=1, device_id=where, device_id_type=MESH)

    greet(device(plane - 1, n, core))
    greet(device(plane - 1, n_x, core))
    greet(device(plane, lax.rem(y + 1, 4) * 2 + x, core))
    greet(device(plane, lax.rem(y + 3, 4) * 2 + x, core))
    greet(device(plane, n_x, core))
    greet(device(plane, n, 1 - core))

    @pl.when(core == 1)
    def _():
        greet(device(plane, n_x, 0))

    def remote(src, dst, send, recv, where):
        return pltpu.make_async_remote_copy(
            src_ref=src,
            dst_ref=dst,
            send_sem=send,
            recv_sem=recv,
            device_id=where,
            device_id_type=MESH,
        )

    def piece(k):
        return pl.ds(HEAD + k * CH, CH) if k else pl.ds(0, HEAD + CH)

    def y_peer(d):
        return device(plane, lax.rem(y + d, 4) * 2 + x, core)

    def y_copy(d, k):
        slot = 2 if d == 1 else 1
        src, dst = r_unit.at[0, piece(k)], r_unit.at[slot, piece(k)]
        return remote(src, dst, y_send.at[slot - 1, k], r_recv.at[slot, k], y_peer(d))

    def relay_copy(slot, k):
        src, dst = r_unit.at[slot, piece(k)], r_unit.at[3, piece(k)]
        where = y_peer(3 if slot == 1 else 1)
        return remote(src, dst, relay_send.at[slot - 1, k % 2], r_recv.at[3, k], where)

    def up(k):
        return pl.ds(*UP[k])

    def p_copy(k):
        src, dst = r_unit.at[0, up(k)], s_unit.at[p_slot, up(k)]
        return remote(src, dst, p_send.at[k], s_recv.at[p_slot, k], device(plane + 1, n_p, core))

    def f_copy(k):
        here = s_unit.at[p_slot, up(k)] if k < LAST else r_unit.at[0, up(k)]
        where = device(plane, n_x, core) if k < LAST else device(plane + 1, n_f, core)
        return remote(here, s_unit.at[f_slot, up(k)], f_send.at[k], s_recv.at[f_slot, k], where)

    def q0_rows(k):
        return up(k) if k == LAST else pl.ds(0, UP[LAST][0])

    def q0_copy(i, k):
        src, dst = r_unit.at[0, q0_rows(k)], s_unit.at[i, q0_rows(k)]
        where = device(plane, n_x if i else n, 1)
        return remote(src, dst, q_send.at[i, k], s_recv.at[i, k], where)

    def q1_copy(i, k):
        src, dst = s_unit.at[2 + i, up(k)], s_unit.at[1 + 2 * i, up(k)]
        where = device(plane, n, 0)
        return remote(src, dst, q_send.at[i, k], s_recv.at[1 + 2 * i, k], where)

    loads[2].wait()
    clusters = jnp.concatenate(
        [ids[...].astype(jnp.float32), jnp.zeros((HEAD - GROUPS, LANES), jnp.float32)], axis=0
    )
    r_unit[0, :HEAD, :LANES] = clusters.astype(jnp.bfloat16)
    r_unit[0, :HEAD, LANES:] = jnp.zeros((HEAD, SK - LANES), jnp.bfloat16)

    def make_units(start, stop):
        sketch = jnp.dot(emb_v[start:stop, :], proj_v[...], preferred_element_type=jnp.float32)
        squares = jnp.sum(sketch * sketch, axis=1, keepdims=True)
        unit = (sketch * lax.rsqrt(squares + 1e-06)).astype(jnp.bfloat16)
        r_unit[0, HEAD + start : HEAD + stop, :] = unit

    loads[0].wait()
    loads[1].wait()
    make_units(0, CH)
    pl.semaphore_wait(barrier, 7 - core)
    p_copy(0).start()
    y_copy(1, 0).start()
    y_copy(3, 0).start()
    loads[3].wait()
    make_units(CH, ROWS)
    p_copy(1).start()
    p_copy(2).start()
    p_copy(3).start()
    p_copy(LAST).start()
    f_copy(LAST).start()
    y_copy(1, 1).start()
    y_copy(3, 2).start()
    y_copy(1, 2).start()
    y_copy(3, 3).start()
    y_copy(1, 3).start()
    y_copy(3, 1).start()

    @pl.when(core == 0)
    def _():
        q0_copy(1, 0).start()

    def clusters_of(unit, slot):
        return unit[slot, :HEAD, :LANES].astype(jnp.float32)

    def columns(slot):
        rows = clusters_of(r_unit, slot)
        for j in range(GROUPS):
            row = jnp.broadcast_to(rows[j : j + 1, :], (LANES, LANES))
            r_col[slot, j * LANES : (j + 1) * LANES, :] = row.T

    columns(0)
    row_acc[...] = jnp.full_like(row_acc, -1.0)

    def landed(ref, sem):
        pltpu.make_async_copy(ref, ref, sem).wait()

    def r_wait(d, k):
        landed(r_unit.at[d, piece(k)], r_recv.at[d, k])

    def s_wait(s, k):
        landed(s_unit.at[s, up(k)], s_recv.at[s, k])

    def to_core_0(i, k):
        @pl.when(core == 1)
        def _():
            q1_copy(i, k).start()

    def hand_on(pieces):
        for k in pieces:
            s_wait(3, k)
            q1_copy(1, k).start()

    def score(r, s, s_clusters, peaks, best):
        scores = lax.dot_general(
            r_unit[r, HEAD:],
            s_unit[s, HEAD:],
            (((1,), (1,)), ((), ())),
            preferred_element_type=jnp.float32,
        )
        a_ids = r_col[r]
        for j in range(GROUPS):
            lanes = slice(j * LANES, (j + 1) * LANES)
            kept = jnp.where(a_ids == s_clusters[j : j + 1, :], scores[:, lanes], -1.0)
            best = jnp.maximum(best, kept)
            peaks[j] = jnp.maximum(peaks[j], jnp.max(kept.reshape(ROWS // 8, 8, LANES), axis=0))
        return best

    def rows_done(r, best):
        at = lax.rem(y + (0, 1, 3, 2)[r], 4)
        for j in range(GROUPS):
            part = best[j * LANES : (j + 1) * LANES, :].T
            row_all[n, at, j : j + 1, :] = jnp.max(part, axis=0, keepdims=True)

    def score_half(r, s, half, s_clusters, peaks, best):
        keys = pl.ds(pl.multiple_of(HEAD + half * (ROWS // 2), HEAD), ROWS // 2)
        scores = lax.dot_general(
            r_unit[r, HEAD:],
            s_unit[s, keys, :],
            (((1,), (1,)), ((), ())),
            preferred_element_type=jnp.float32,
        )
        a_ids = r_col[r]
        for j in range(GROUPS // 2):
            b_ids = jnp.where(half == 0, s_clusters[j : j + 1, :], s_clusters[j + 2 : j + 3, :])
            kept = jnp.where(a_ids == b_ids, scores[:, j * LANES : (j + 1) * LANES], -1.0)
            best = jnp.maximum(best, kept)
            peaks[j] = jnp.maximum(peaks[j], jnp.max(kept.reshape(ROWS // 8, 8, LANES), axis=0))
        return best

    def half_slot(s, half, done):
        s_clusters = clusters_of(s_unit, s)
        peaks = empty()[: GROUPS // 2]
        for r in range(4):
            done(r, score_half(r, s, half, s_clusters, peaks, row_acc[r]))
        for j in range(GROUPS // 2):
            col_acc[s, half * 2 + j] = peaks[j]

    def keep(r, best):
        row_acc[r] = best

    def score_near(s, peaks):
        s_clusters = clusters_of(s_unit, s)
        for r in range(3):
            row_acc[r] = score(r, s, s_clusters, peaks, row_acc[r])

    def empty():
        return [jnp.full((8, LANES), -1.0, jnp.float32)] * GROUPS

    def up_and_over(pieces):
        for k in pieces:
            s_wait(p_slot, k)
            f_copy(k).start()
            to_core_0(0, k)

    def tell(sem, where):
        pl.semaphore_signal(sem, inc=1, device_id=where, device_id_type=MESH)

    def say_ready():
        pl.semaphore_wait(seen, 1)
        tell(ready, device(plane + 1, n_p, core))

    def on_core(which, pieces, act):
        @pl.when(core == which)
        def _():
            for k in pieces:
                act(k)

    def relay(k):
        for slot, piece_of in ((2, k), (1, 2 + k)):
            r_wait(slot, piece_of)
            relay_copy(slot, piece_of).start()

    def late_q0():
        for i in (1, 0):
            q0_copy(i, LAST).start()
        q0_copy(0, 0).start()

    def r_wait_near():
        for k in range(2):
            r_wait(1, k)
            r_wait(2, 2 + k)
        columns(1)
        columns(2)

    def r_wait_far():
        for k in range(CHUNKS):
            r_wait(3, k)
        columns(3)

    def q0_wait(s):
        for k in (0, LAST):
            landed(s_unit.at[s, q0_rows(k)], s_recv.at[s, k])

    @pl.when(crosses_in)
    def _():
        relay(0)
        tell(seen, device(plane, n_x, core))
        on_core(0, (0,), lambda _: late_q0())
        relay(1)
        say_ready()

        @pl.loop(0, 7)
        def _(i):
            @pl.when(i == 0)
            def _():
                up_and_over((0, 1))
                r_wait_near()
                r_wait_far()
                on_core(1, (0, 1), q0_wait)

            @pl.when(i == 1)
            def _():
                up_and_over((2, 3))
                on_core(0, (0, 1), lambda k: s_wait(1, k))

            @pl.when(i == 2)
            def _():
                s_wait(f_slot, 0)
                to_core_0(1, 0)
                on_core(0, (LAST,), lambda k: s_wait(0, k))

            @pl.when(i == 3)
            def _():
                on_core(0, (2, 3, LAST), lambda k: s_wait(1, k))
                on_core(1, (LAST,), lambda k: s_wait(2, k))
                to_core_0(0, LAST)

            @pl.when(i == 4)
            def _():
                on_core(0, (1,), lambda k: s_wait(2, k))

            @pl.when(i == 5)
            def _():
                on_core(0, (0, 1), lambda k: s_wait(3, k))
                on_core(1, (0,), lambda _: hand_on((1, 2)))

            @pl.when(i == 6)
            def _():
                on_core(0, (2, 3, LAST), lambda k: s_wait(2, k))
                on_core(1, (0,), lambda _: hand_on((3,)))
                on_core(1, (0,), lambda _: pl.semaphore_wait(ready, 1))
                on_core(1, (0,), lambda _: hand_on((LAST,)))

            s = jnp.where(core == 0, 2 * (i // 4) + lax.rem(i, 2), i // 2)
            half = jnp.where(core == 0, lax.rem(i, 4) // 2, lax.rem(i, 2))
            half_slot(s, half, keep)

        on_core(0, (2, 3, LAST), lambda k: s_wait(3, k))
        half_slot(3, 1, rows_done)

    @pl.when(jnp.logical_not(crosses_in))
    def _():
        relay(0)
        tell(seen, device(plane, n_x, core))
        up_and_over((0,))
        on_core(0, (0,), lambda _: late_q0())
        up_and_over((1,))
        relay(1)
        up_and_over((2, 3))
        say_ready()
        s_wait(f_slot, 0)
        to_core_0(1, 0)
        s_wait(p_slot, LAST)
        to_core_0(0, LAST)
        r_wait_near()

        @pl.loop(0, 2)
        def _(s):
            @pl.when(jnp.logical_and(core == 0, s == 1))
            def _():
                for k in range(LAST + 1):
                    s_wait(1, k)

            @pl.when(core == 1)
            def _():
                q0_wait(s)

            peaks = empty()
            score_near(s, peaks)
            for j in range(GROUPS):
                col_acc[s, j] = peaks[j]

        @pl.when(core == 1)
        def _():
            hand_on((1, 2))

        r_wait_far()
        best = row_acc[3]
        for s in range(2):
            peaks = [col_acc[s, j] for j in range(GROUPS)]
            best = score(3, s, clusters_of(s_unit, s), peaks, best)
            for j in range(GROUPS):
                col_acc[s, j] = peaks[j]
        row_acc[3] = best

        @pl.when(core == 0)
        def _():
            for k in range(1, LAST + 1):
                s_wait(2, k)

        @pl.when(core == 1)
        def _():
            hand_on((3,))
            pl.semaphore_wait(ready, 1)
            hand_on((LAST,))

        peaks = empty()
        score_near(2, peaks)
        row_acc[3] = score(3, 2, clusters_of(s_unit, 2), peaks, row_acc[3])
        for j in range(GROUPS):
            col_acc[2, j] = peaks[j]

        @pl.when(core == 0)
        def _():
            for k in range(LAST + 1):
                s_wait(3, k)

        s_clusters = clusters_of(s_unit, 3)
        peaks = empty()
        for r in range(4):
            rows_done(r, score(r, 3, s_clusters, peaks, row_acc[r]))
        for j in range(GROUPS):
            col_acc[3, j] = peaks[j]

    def tail(src, dst, kind, where):
        return remote(src, dst, tail_send.at[kind], tail_recv.at[kind], where)

    def send_rows():
        for m in (
            *(device(plane, lax.rem(y + d, 4) * 2 + 1 - x, core) for d in (2, 1, 3)),
            *(y_peer(d) for d in (2, 1, 3)),
            device(plane, n_x, core),
        ):
            tail(row_all.at[n], row_all.at[n], 0, m).start()

    @pl.when(crosses_in)
    def _():
        send_rows()

    for s in range(4):
        block = jnp.where(core == 0, s % 2, 1 - s // 2)
        x_0 = x_p if s < 2 else 1 - x_p
        x_1 = (x, 1 - x, x_p, 1 - x_p)[s]
        x_abs = jnp.where(core == 0, x_0, x_1)
        for j in range(GROUPS):
            peak = jnp.max(col_acc[s, j], axis=0, keepdims=True)
            col_src[block, x_abs, j : j + 1, :] = peak

    @pl.when(core == 0)
    def _():
        pl.semaphore_wait(ready, 1)

    for k in range(8):
        tail(col_src.at[0], col_all.at[0, n], 1, device(plane - 1, k, core)).start()
        tail(col_src.at[1], col_all.at[1, n], 1, device(plane - 1 + core, k, 1 - core)).start()

    @pl.when(jnp.logical_not(crosses_in))
    def _():
        send_rows()

    for k in range(CHUNKS):
        y_copy(1, k).wait_send()
        y_copy(3, k).wait_send()
        relay_copy(1 if k >= 2 else 2, k).wait_send()
    for k in range(LAST + 1):
        p_copy(k).wait_send()
        f_copy(k).wait_send()
    for i in range(2):

        @pl.when(core == 0)
        def _():
            q0_copy(i, 0).wait_send()
            q0_copy(i, LAST).wait_send()

        @pl.when(core == 1)
        def _():
            for k in range(LAST + 1):
                q1_copy(i, k).wait_send()

    some = row_all.at[pl.ds(0, 7)]
    landed(some, tail_recv.at[0])
    landed(col_all, tail_recv.at[1])
    for y_abs in range(4):
        for x_abs in range(2):
            best = jnp.full((GROUPS, LANES), -1.0, jnp.float32)
            for y_from in range(4):
                best = jnp.maximum(best, row_all[y_from * 2 + x_abs, y_abs])
            for g in range(2):
                for x_from in range(2):
                    best = jnp.maximum(best, col_all[g, y_abs * 2 + x_from, x_abs])
            out[y_abs * 2 + x_abs] = best

    landed(some, tail_send.at[0])
    landed(col_all, tail_send.at[1])


def body(embeddings, projection, cluster_id):
    dma = pltpu.SemaphoreType.DMA
    operands = embeddings, projection, cluster_id.reshape(GROUPS, LANES)
    best = pl.pallas_call(
        kernel,
        out_shape=jax.ShapeDtypeStruct((8, GROUPS, LANES), jnp.float32),
        in_specs=[
            pl.BlockSpec(memory_space=pltpu.HBM),
            pl.BlockSpec(memory_space=pltpu.HBM),
            pl.BlockSpec(memory_space=pltpu.HBM),
        ],
        out_specs=pl.BlockSpec(memory_space=pltpu.VMEM),
        scratch_shapes=[
            pltpu.VMEM((ROWS, D), jnp.bfloat16),
            pltpu.VMEM((D, SK), jnp.bfloat16),
            pltpu.VMEM((GROUPS, LANES), jnp.int32),
            pltpu.VMEM((4, HEAD + ROWS, SK), jnp.bfloat16),
            pltpu.VMEM((4, HEAD + ROWS, SK), jnp.bfloat16),
            pltpu.VMEM((4, ROWS, LANES), jnp.float32),
            pltpu.VMEM((4, ROWS, LANES), jnp.float32),
            pltpu.VMEM((4, GROUPS, 8, LANES), jnp.float32),
            pltpu.VMEM((8, 4, GROUPS, LANES), jnp.float32),
            pltpu.VMEM((2, 2, GROUPS, LANES), jnp.float32),
            pltpu.VMEM((2, 8, 2, GROUPS, LANES), jnp.float32),
            dma((4,)),
            dma((2, CHUNKS)),
            dma((2, 2)),
            dma((4, CHUNKS)),
            dma((LAST + 1,)),
            dma((LAST + 1,)),
            dma((2, LAST + 1)),
            dma((4, LAST + 1)),
            dma((2,)),
            dma((2,)),
            pltpu.SemaphoreType.REGULAR,
            pltpu.SemaphoreType.REGULAR,
        ],
        compiler_params=pltpu.CompilerParams(
            collective_id=0, has_side_effects=True, vmem_limit_bytes=32 << 20
        ),
        name="best_match",
    )(*(pltpu.with_memory_space_constraint(a, pltpu.HBM) for a in operands))
    return best.reshape(8 * ROWS)


def solution(mesh):
    in_specs = (P(("wide", "narrow"), None), P(), P(("wide", "narrow")))
    out_specs = P("wide")
    return jax.shard_map(body, mesh=mesh, in_specs=in_specs, out_specs=out_specs, check_vma=False)
```

```python
import jax
import jax.numpy as jnp
from jax import lax
from jax.experimental import pallas as pl
from jax.experimental.pallas import tpu as pltpu
from jax.sharding import PartitionSpec as P

MESH = pl.DeviceIdType.MESH
ROWS = 512
SK = 256
D = 1024
CHUNKS = 4
CH = ROWS // CHUNKS
HEAD = 16
UP = ((0, 144), (144, 128), (272, 96), (368, 64), (432, 96))
LAST = len(UP) - 1
PLANES = 16
LANES = 128
GROUPS = ROWS // LANES


def device(plane, n, core):
    return (lax.rem(plane + PLANES, PLANES) * 2 + core, n)


def kernel(
    emb,
    proj,
    ids_in,
    out,
    emb_v,
    proj_v,
    ids,
    r_unit,
    s_unit,
    r_col,
    row_acc,
    col_acc,
    row_all,
    col_src,
    col_all,
    in_sem,
    y_send,
    relay_send,
    r_recv,
    p_send,
    f_send,
    q_send,
    s_recv,
    tail_send,
    tail_recv,
    ready,
    seen,
):
    wide, n = lax.axis_index("wide"), lax.axis_index("narrow")
    plane, core = wide // 2, lax.rem(wide, 2)
    y, x = n // 2, lax.rem(n, 2)
    n_x = y * 2 + 1 - x
    crosses_out = lax.rem(plane, 8) == 7
    crosses_in = lax.rem(plane, 8) == 0
    n_p = jnp.where(crosses_out, n_x, n)
    n_f = jnp.where(crosses_out, n, n_x)
    x_p = jnp.where(crosses_in, 1 - x, x)
    p_slot, f_slot = 2 * core, 2 + core

    first, rest = pl.ds(0, CH), pl.ds(CH, ROWS - CH)
    loads = [
        pltpu.make_async_copy(proj, proj_v, in_sem.at[0]),
        pltpu.make_async_copy(emb.at[first], emb_v.at[first], in_sem.at[1]),
        pltpu.make_async_copy(ids_in, ids, in_sem.at[2]),
        pltpu.make_async_copy(emb.at[rest], emb_v.at[rest], in_sem.at[3]),
    ]
    for copy in loads:
        copy.start()

    barrier = pltpu.get_barrier_semaphore()

    def greet(where):
        pl.semaphore_signal(barrier, inc=1, device_id=where, device_id_type=MESH)

    greet(device(plane - 1, n, core))
    greet(device(plane - 1, n_x, core))
    greet(device(plane, lax.rem(y + 1, 4) * 2 + x, core))
    greet(device(plane, lax.rem(y + 3, 4) * 2 + x, core))
    greet(device(plane, n_x, core))
    greet(device(plane, n, 1 - core))

    @pl.when(core == 1)
    def _():
        greet(device(plane, n_x, 0))

    def remote(src, dst, send, recv, where):
        return pltpu.make_async_remote_copy(
            src_ref=src,
            dst_ref=dst,
            send_sem=send,
            recv_sem=recv,
            device_id=where,
            device_id_type=MESH,
        )

    def piece(k):
        return pl.ds(HEAD + k * CH, CH) if k else pl.ds(0, HEAD + CH)

    def y_peer(d):
        return device(plane, lax.rem(y + d, 4) * 2 + x, core)

    def y_copy(d, k):
        slot = 2 if d == 1 else 1
        src, dst = r_unit.at[0, piece(k)], r_unit.at[slot, piece(k)]
        return remote(src, dst, y_send.at[slot - 1, k], r_recv.at[slot, k], y_peer(d))

    def relay_copy(slot, k):
        src, dst = r_unit.at[slot, piece(k)], r_unit.at[3, piece(k)]
        where = y_peer(3 if slot == 1 else 1)
        return remote(src, dst, relay_send.at[slot - 1, k % 2], r_recv.at[3, k], where)

    def up(k):
        return pl.ds(*UP[k])

    def p_copy(k):
        src, dst = r_unit.at[0, up(k)], s_unit.at[p_slot, up(k)]
        return remote(src, dst, p_send.at[k], s_recv.at[p_slot, k], device(plane + 1, n_p, core))

    def f_copy(k):
        here = s_unit.at[p_slot, up(k)] if k < LAST else r_unit.at[0, up(k)]
        where = device(plane, n_x, core) if k < LAST else device(plane + 1, n_f, core)
        return remote(here, s_unit.at[f_slot, up(k)], f_send.at[k], s_recv.at[f_slot, k], where)

    def q0_rows(k):
        return up(k) if k == LAST else pl.ds(0, UP[LAST][0])

    def q0_copy(i, k):
        src, dst = r_unit.at[0, q0_rows(k)], s_unit.at[i, q0_rows(k)]
        where = device(plane, n_x if i else n, 1)
        return remote(src, dst, q_send.at[i, k], s_recv.at[i, k], where)

    def q1_copy(i, k):
        src, dst = s_unit.at[2 + i, up(k)], s_unit.at[1 + 2 * i, up(k)]
        where = device(plane, n, 0)
        return remote(src, dst, q_send.at[i, k], s_recv.at[1 + 2 * i, k], where)

    loads[2].wait()
    clusters = jnp.concatenate(
        [ids[...].astype(jnp.float32), jnp.zeros((HEAD - GROUPS, LANES), jnp.float32)], axis=0
    )
    r_unit[0, :HEAD, :LANES] = clusters.astype(jnp.bfloat16)
    r_unit[0, :HEAD, LANES:] = jnp.zeros((HEAD, SK - LANES), jnp.bfloat16)

    def make_units(start, stop):
        sketch = jnp.dot(emb_v[start:stop, :], proj_v[...], preferred_element_type=jnp.float32)
        squares = jnp.sum(sketch * sketch, axis=1, keepdims=True)
        unit = (sketch * lax.rsqrt(squares + 1e-06)).astype(jnp.bfloat16)
        r_unit[0, HEAD + start : HEAD + stop, :] = unit

    loads[0].wait()
    loads[1].wait()
    make_units(0, CH)
    pl.semaphore_wait(barrier, 7 - core)
    p_copy(0).start()
    y_copy(1, 0).start()
    y_copy(3, 0).start()
    loads[3].wait()
    make_units(CH, ROWS)
    p_copy(1).start()
    p_copy(2).start()
    p_copy(3).start()
    p_copy(LAST).start()
    f_copy(LAST).start()
    y_copy(1, 1).start()
    y_copy(3, 2).start()
    y_copy(1, 2).start()
    y_copy(3, 3).start()
    y_copy(1, 3).start()
    y_copy(3, 1).start()

    @pl.when(core == 0)
    def _():
        q0_copy(1, 0).start()

    def clusters_of(unit, slot):
        return unit[slot, :HEAD, :LANES].astype(jnp.float32)

    def columns(slot):
        rows = clusters_of(r_unit, slot)
        for j in range(GROUPS):
            row = jnp.broadcast_to(rows[j : j + 1, :], (LANES, LANES))
            r_col[slot, j * LANES : (j + 1) * LANES, :] = row.T

    columns(0)
    row_acc[...] = jnp.full_like(row_acc, -1.0)

    def landed(ref, sem):
        pltpu.make_async_copy(ref, ref, sem).wait()

    def r_wait(d, k):
        landed(r_unit.at[d, piece(k)], r_recv.at[d, k])

    def s_wait(s, k):
        landed(s_unit.at[s, up(k)], s_recv.at[s, k])

    def to_core_0(i, k):
        @pl.when(core == 1)
        def _():
            q1_copy(i, k).start()

    def hand_on(pieces):
        for k in pieces:
            s_wait(3, k)
            q1_copy(1, k).start()

    def score(r, s, s_clusters, peaks, best):
        scores = lax.dot_general(
            r_unit[r, HEAD:],
            s_unit[s, HEAD:],
            (((1,), (1,)), ((), ())),
            preferred_element_type=jnp.float32,
        )
        a_ids = r_col[r]
        for j in range(GROUPS):
            lanes = slice(j * LANES, (j + 1) * LANES)
            kept = jnp.where(a_ids == s_clusters[j : j + 1, :], scores[:, lanes], -1.0)
            best = jnp.maximum(best, kept)
            peaks[j] = jnp.maximum(peaks[j], jnp.max(kept.reshape(ROWS // 8, 8, LANES), axis=0))
        return best

    def rows_done(r, best):
        at = lax.rem(y + (0, 1, 3, 2)[r], 4)
        for j in range(GROUPS):
            part = best[j * LANES : (j + 1) * LANES, :].T
            row_all[n, at, j : j + 1, :] = jnp.max(part, axis=0, keepdims=True)

    def score_half(r, s, half, s_clusters, peaks, best):
        keys = pl.ds(pl.multiple_of(HEAD + half * (ROWS // 2), HEAD), ROWS // 2)
        scores = lax.dot_general(
            r_unit[r, HEAD:],
            s_unit[s, keys, :],
            (((1,), (1,)), ((), ())),
            preferred_element_type=jnp.float32,
        )
        a_ids = r_col[r]
        for j in range(GROUPS // 2):
            b_ids = jnp.where(half == 0, s_clusters[j : j + 1, :], s_clusters[j + 2 : j + 3, :])
            kept = jnp.where(a_ids == b_ids, scores[:, j * LANES : (j + 1) * LANES], -1.0)
            best = jnp.maximum(best, kept)
            peaks[j] = jnp.maximum(peaks[j], jnp.max(kept.reshape(ROWS // 8, 8, LANES), axis=0))
        return best

    def half_slot(s, half, done):
        s_clusters = clusters_of(s_unit, s)
        peaks = empty()[: GROUPS // 2]
        for r in range(4):
            done(r, score_half(r, s, half, s_clusters, peaks, row_acc[r]))
        for j in range(GROUPS // 2):
            col_acc[s, half * 2 + j] = peaks[j]

    def keep(r, best):
        row_acc[r] = best

    def score_near(s, peaks):
        s_clusters = clusters_of(s_unit, s)
        for r in range(3):
            row_acc[r] = score(r, s, s_clusters, peaks, row_acc[r])

    def empty():
        return [jnp.full((8, LANES), -1.0, jnp.float32)] * GROUPS

    def up_and_over(pieces):
        for k in pieces:
            s_wait(p_slot, k)
            f_copy(k).start()
            to_core_0(0, k)

    def tell(sem, where):
        pl.semaphore_signal(sem, inc=1, device_id=where, device_id_type=MESH)

    def say_ready():
        pl.semaphore_wait(seen, 1)
        tell(ready, device(plane + 1, n_p, core))

    def on_core(which, pieces, act):
        @pl.when(core == which)
        def _():
            for k in pieces:
                act(k)

    def relay(k):
        for slot, piece_of in ((2, k), (1, 2 + k)):
            r_wait(slot, piece_of)
            relay_copy(slot, piece_of).start()

    def late_q0():
        for i in (1, 0):
            q0_copy(i, LAST).start()
        q0_copy(0, 0).start()

    def r_wait_near():
        for k in range(2):
            r_wait(1, k)
            r_wait(2, 2 + k)
        columns(1)
        columns(2)

    def r_wait_far():
        for k in range(CHUNKS):
            r_wait(3, k)
        columns(3)

    def q0_wait(s):
        for k in (0, LAST):
            landed(s_unit.at[s, q0_rows(k)], s_recv.at[s, k])

    @pl.when(crosses_in)
    def _():
        relay(0)
        tell(seen, device(plane, n_x, core))
        on_core(0, (0,), lambda _: late_q0())
        relay(1)
        say_ready()

        @pl.loop(0, 6)
        def _(i):
            @pl.when(i == 0)
            def _():
                up_and_over((0, 1))
                r_wait_near()
                r_wait_far()
                on_core(1, (0, 1), q0_wait)

            @pl.when(i == 1)
            def _():
                up_and_over((2, 3))
                on_core(0, (0, 1), lambda k: s_wait(1, k))

            @pl.when(i == 2)
            def _():
                s_wait(f_slot, 0)
                to_core_0(1, 0)
                on_core(0, (LAST,), lambda k: s_wait(0, k))

            @pl.when(i == 3)
            def _():
                on_core(0, (2, 3, LAST), lambda k: s_wait(1, k))
                on_core(1, (LAST,), lambda k: s_wait(2, k))
                to_core_0(0, LAST)

            @pl.when(i == 4)
            def _():
                on_core(0, (1,), lambda k: s_wait(2, k))

            @pl.when(i == 5)
            def _():
                on_core(0, (0, 1), lambda k: s_wait(3, k))
                on_core(1, (0,), lambda _: hand_on((1, 2)))

            by_slot = jnp.logical_and(core == 1, i < 4)
            s = jnp.where(by_slot, i // 2, 2 * (i // 4) + lax.rem(i, 2))
            half = jnp.where(by_slot, lax.rem(i, 2), lax.rem(i, 4) // 2)
            half_slot(s, half, keep)

        on_core(1, (0,), lambda _: hand_on((3,)))
        on_core(1, (0,), lambda _: pl.semaphore_wait(ready, 1))
        on_core(1, (0,), lambda _: hand_on((LAST,)))
        for slot in (2, 3):
            on_core(0, (2, 3, LAST), lambda k, slot=slot: s_wait(slot, k))
        peaks = [empty()[: GROUPS // 2] for _ in range(2)]
        clusters_2, clusters_3 = clusters_of(s_unit, 2), clusters_of(s_unit, 3)
        for r in range(4):
            best = score_half(r, 2, 1, clusters_2, peaks[0], row_acc[r])
            rows_done(r, score_half(r, 3, 1, clusters_3, peaks[1], best))
        for i in range(2):
            for j in range(GROUPS // 2):
                col_acc[2 + i, 2 + j] = peaks[i][j]

    @pl.when(jnp.logical_not(crosses_in))
    def _():
        relay(0)
        tell(seen, device(plane, n_x, core))
        up_and_over((0,))
        on_core(0, (0,), lambda _: late_q0())
        up_and_over((1,))
        relay(1)
        up_and_over((2, 3))
        say_ready()
        s_wait(f_slot, 0)
        to_core_0(1, 0)
        s_wait(p_slot, LAST)
        to_core_0(0, LAST)
        r_wait_near()

        @pl.loop(0, 2)
        def _(s):
            @pl.when(jnp.logical_and(core == 0, s == 1))
            def _():
                for k in range(LAST + 1):
                    s_wait(1, k)

            @pl.when(core == 1)
            def _():
                q0_wait(s)

            peaks = empty()
            score_near(s, peaks)
            for j in range(GROUPS):
                col_acc[s, j] = peaks[j]

        @pl.when(core == 1)
        def _():
            hand_on((1, 2))

        r_wait_far()
        best = row_acc[3]
        for s in range(2):
            peaks = [col_acc[s, j] for j in range(GROUPS)]
            best = score(3, s, clusters_of(s_unit, s), peaks, best)
            for j in range(GROUPS):
                col_acc[s, j] = peaks[j]
        row_acc[3] = best

        @pl.when(core == 0)
        def _():
            for k in range(1, LAST + 1):
                s_wait(2, k)

        @pl.when(core == 1)
        def _():
            hand_on((3,))
            pl.semaphore_wait(ready, 1)
            hand_on((LAST,))

        peaks = empty()
        score_near(2, peaks)
        row_acc[3] = score(3, 2, clusters_of(s_unit, 2), peaks, row_acc[3])
        for j in range(GROUPS):
            col_acc[2, j] = peaks[j]

        @pl.when(core == 0)
        def _():
            for k in range(LAST + 1):
                s_wait(3, k)

        s_clusters = clusters_of(s_unit, 3)
        peaks = empty()
        for r in range(4):
            rows_done(r, score(r, 3, s_clusters, peaks, row_acc[r]))
        for j in range(GROUPS):
            col_acc[3, j] = peaks[j]

    def tail(src, dst, kind, where):
        return remote(src, dst, tail_send.at[kind], tail_recv.at[kind], where)

    def send_rows():
        for m in (
            *(device(plane, lax.rem(y + d, 4) * 2 + 1 - x, core) for d in (2, 1, 3)),
            *(y_peer(d) for d in (2, 1, 3)),
            device(plane, n_x, core),
        ):
            tail(row_all.at[n], row_all.at[n], 0, m).start()

    send_rows()

    for s in range(4):
        block = jnp.where(core == 0, s % 2, 1 - s // 2)
        x_0 = x_p if s < 2 else 1 - x_p
        x_1 = (x, 1 - x, x_p, 1 - x_p)[s]
        x_abs = jnp.where(core == 0, x_0, x_1)
        for j in range(GROUPS):
            peak = jnp.max(col_acc[s, j], axis=0, keepdims=True)
            col_src[block, x_abs, j : j + 1, :] = peak

    @pl.when(core == 0)
    def _():
        pl.semaphore_wait(ready, 1)

    for k in range(8):
        tail(col_src.at[0], col_all.at[0, n], 1, device(plane - 1, k, core)).start()
        tail(col_src.at[1], col_all.at[1, n], 1, device(plane - 1 + core, k, 1 - core)).start()


    for k in range(CHUNKS):
        y_copy(1, k).wait_send()
        y_copy(3, k).wait_send()
        relay_copy(1 if k >= 2 else 2, k).wait_send()
    for k in range(LAST + 1):
        p_copy(k).wait_send()
        f_copy(k).wait_send()
    for i in range(2):

        @pl.when(core == 0)
        def _():
            q0_copy(i, 0).wait_send()
            q0_copy(i, LAST).wait_send()

        @pl.when(core == 1)
        def _():
            for k in range(LAST + 1):
                q1_copy(i, k).wait_send()

    some = row_all.at[pl.ds(0, 7)]
    landed(some, tail_recv.at[0])
    landed(col_all, tail_recv.at[1])
    for y_abs in range(4):
        for x_abs in range(2):
            best = jnp.full((GROUPS, LANES), -1.0, jnp.float32)
            for y_from in range(4):
                best = jnp.maximum(best, row_all[y_from * 2 + x_abs, y_abs])
            for g in range(2):
                for x_from in range(2):
                    best = jnp.maximum(best, col_all[g, y_abs * 2 + x_from, x_abs])
            out[y_abs * 2 + x_abs] = best

    landed(some, tail_send.at[0])
    landed(col_all, tail_send.at[1])


def body(embeddings, projection, cluster_id):
    dma = pltpu.SemaphoreType.DMA
    operands = embeddings, projection, cluster_id.reshape(GROUPS, LANES)
    best = pl.pallas_call(
        kernel,
        out_shape=jax.ShapeDtypeStruct((8, GROUPS, LANES), jnp.float32),
        in_specs=[
            pl.BlockSpec(memory_space=pltpu.HBM),
            pl.BlockSpec(memory_space=pltpu.HBM),
            pl.BlockSpec(memory_space=pltpu.HBM),
        ],
        out_specs=pl.BlockSpec(memory_space=pltpu.VMEM),
        scratch_shapes=[
            pltpu.VMEM((ROWS, D), jnp.bfloat16),
            pltpu.VMEM((D, SK), jnp.bfloat16),
            pltpu.VMEM((GROUPS, LANES), jnp.int32),
            pltpu.VMEM((4, HEAD + ROWS, SK), jnp.bfloat16),
            pltpu.VMEM((4, HEAD + ROWS, SK), jnp.bfloat16),
            pltpu.VMEM((4, ROWS, LANES), jnp.float32),
            pltpu.VMEM((4, ROWS, LANES), jnp.float32),
            pltpu.VMEM((4, GROUPS, 8, LANES), jnp.float32),
            pltpu.VMEM((8, 4, GROUPS, LANES), jnp.float32),
            pltpu.VMEM((2, 2, GROUPS, LANES), jnp.float32),
            pltpu.VMEM((2, 8, 2, GROUPS, LANES), jnp.float32),
            dma((4,)),
            dma((2, CHUNKS)),
            dma((2, 2)),
            dma((4, CHUNKS)),
            dma((LAST + 1,)),
            dma((LAST + 1,)),
            dma((2, LAST + 1)),
            dma((4, LAST + 1)),
            dma((2,)),
            dma((2,)),
            pltpu.SemaphoreType.REGULAR,
            pltpu.SemaphoreType.REGULAR,
        ],
        compiler_params=pltpu.CompilerParams(
            collective_id=0, has_side_effects=True, vmem_limit_bytes=32 << 20
        ),
        name="best_match",
    )(*(pltpu.with_memory_space_constraint(a, pltpu.HBM) for a in operands))
    return best.reshape(8 * ROWS)


def solution(mesh):
    in_specs = (P(("wide", "narrow"), None), P(), P(("wide", "narrow")))
    out_specs = P("wide")
    return jax.shard_map(body, mesh=mesh, in_specs=in_specs, out_specs=out_specs, check_vma=False)
```

```python
import jax
import jax.numpy as jnp
from jax import lax
from jax.experimental import pallas as pl
from jax.experimental.pallas import tpu as pltpu
from jax.sharding import PartitionSpec as P

MESH = pl.DeviceIdType.MESH
ROWS = 512
SK = 256
D = 1024
CHUNKS = 4
CH = ROWS // CHUNKS
HEAD = 16
UP = ((0, 144), (144, 128), (272, 96), (368, 64), (432, 96))
LAST = len(UP) - 1
PLANES = 16
LANES = 128
GROUPS = ROWS // LANES


def device(plane, n, core):
    return (lax.rem(plane + PLANES, PLANES) * 2 + core, n)


def kernel(
    emb,
    proj,
    ids_in,
    out,
    emb_v,
    proj_v,
    ids,
    r_unit,
    s_unit,
    r_col,
    row_acc,
    col_acc,
    row_all,
    col_src,
    col_all,
    in_sem,
    y_send,
    relay_send,
    r_recv,
    p_send,
    f_send,
    q_send,
    s_recv,
    tail_send,
    tail_recv,
    ready,
    seen,
):
    wide, n = lax.axis_index("wide"), lax.axis_index("narrow")
    plane, core = wide // 2, lax.rem(wide, 2)
    y, x = n // 2, lax.rem(n, 2)
    n_x = y * 2 + 1 - x
    crosses_out = lax.rem(plane, 8) == 7
    crosses_in = lax.rem(plane, 8) == 0
    n_p = jnp.where(crosses_out, n_x, n)
    n_f = jnp.where(crosses_out, n, n_x)
    x_p = jnp.where(crosses_in, 1 - x, x)
    p_slot, f_slot = 2 * core, 2 + core

    first, rest = pl.ds(0, CH), pl.ds(CH, ROWS - CH)
    loads = [
        pltpu.make_async_copy(proj, proj_v, in_sem.at[0]),
        pltpu.make_async_copy(emb.at[first], emb_v.at[first], in_sem.at[1]),
        pltpu.make_async_copy(ids_in, ids, in_sem.at[2]),
        pltpu.make_async_copy(emb.at[rest], emb_v.at[rest], in_sem.at[3]),
    ]
    for copy in loads:
        copy.start()

    barrier = pltpu.get_barrier_semaphore()

    def greet(where):
        pl.semaphore_signal(barrier, inc=1, device_id=where, device_id_type=MESH)

    greet(device(plane - 1, n, core))
    greet(device(plane - 1, n_x, core))
    greet(device(plane, lax.rem(y + 1, 4) * 2 + x, core))
    greet(device(plane, lax.rem(y + 3, 4) * 2 + x, core))
    greet(device(plane, n_x, core))
    greet(device(plane, n, 1 - core))

    @pl.when(core == 1)
    def _():
        greet(device(plane, n_x, 0))

    def remote(src, dst, send, recv, where):
        return pltpu.make_async_remote_copy(
            src_ref=src,
            dst_ref=dst,
            send_sem=send,
            recv_sem=recv,
            device_id=where,
            device_id_type=MESH,
        )

    def piece(k):
        return pl.ds(HEAD + k * CH, CH) if k else pl.ds(0, HEAD + CH)

    def y_peer(d):
        return device(plane, lax.rem(y + d, 4) * 2 + x, core)

    def y_copy(d, k):
        slot = 2 if d == 1 else 1
        src, dst = r_unit.at[0, piece(k)], r_unit.at[slot, piece(k)]
        return remote(src, dst, y_send.at[slot - 1, k], r_recv.at[slot, k], y_peer(d))

    def relay_copy(slot, k):
        src, dst = r_unit.at[slot, piece(k)], r_unit.at[3, piece(k)]
        where = y_peer(3 if slot == 1 else 1)
        return remote(src, dst, relay_send.at[slot - 1, k % 2], r_recv.at[3, k], where)

    def up(k):
        return pl.ds(*UP[k])

    def p_copy(k):
        src, dst = r_unit.at[0, up(k)], s_unit.at[p_slot, up(k)]
        return remote(src, dst, p_send.at[k], s_recv.at[p_slot, k], device(plane + 1, n_p, core))

    def f_copy(k):
        here = s_unit.at[p_slot, up(k)] if k < LAST else r_unit.at[0, up(k)]
        where = device(plane, n_x, core) if k < LAST else device(plane + 1, n_f, core)
        return remote(here, s_unit.at[f_slot, up(k)], f_send.at[k], s_recv.at[f_slot, k], where)

    def q0_rows(k):
        return up(k) if k == LAST else pl.ds(0, UP[LAST][0])

    def q0_copy(i, k):
        src, dst = r_unit.at[0, q0_rows(k)], s_unit.at[i, q0_rows(k)]
        where = device(plane, n_x if i else n, 1)
        return remote(src, dst, q_send.at[i, k], s_recv.at[i, k], where)

    def q1_copy(i, k):
        src, dst = s_unit.at[2 + i, up(k)], s_unit.at[1 + 2 * i, up(k)]
        where = device(plane, n, 0)
        return remote(src, dst, q_send.at[i, k], s_recv.at[1 + 2 * i, k], where)

    loads[2].wait()
    clusters = jnp.concatenate(
        [ids[...].astype(jnp.float32), jnp.zeros((HEAD - GROUPS, LANES), jnp.float32)], axis=0
    )
    r_unit[0, :HEAD, :LANES] = clusters.astype(jnp.bfloat16)
    r_unit[0, :HEAD, LANES:] = jnp.zeros((HEAD, SK - LANES), jnp.bfloat16)

    def make_units(start, stop):
        sketch = jnp.dot(emb_v[start:stop, :], proj_v[...], preferred_element_type=jnp.float32)
        squares = jnp.sum(sketch * sketch, axis=1, keepdims=True)
        unit = (sketch * lax.rsqrt(squares + 1e-06)).astype(jnp.bfloat16)
        r_unit[0, HEAD + start : HEAD + stop, :] = unit

    loads[0].wait()
    loads[1].wait()
    make_units(0, CH)
    pl.semaphore_wait(barrier, 7 - core)
    p_copy(0).start()
    y_copy(1, 0).start()
    loads[3].wait()
    make_units(CH, ROWS)
    p_copy(1).start()
    p_copy(2).start()
    p_copy(3).start()
    p_copy(LAST).start()
    f_copy(LAST).start()
    y_copy(3, 2).start()
    y_copy(1, 1).start()
    y_copy(3, 3).start()
    y_copy(1, 2).start()
    y_copy(3, 0).start()
    y_copy(1, 3).start()
    y_copy(3, 1).start()

    @pl.when(core == 0)
    def _():
        q0_copy(1, 0).start()

    def clusters_of(unit, slot):
        return unit[slot, :HEAD, :LANES].astype(jnp.float32)

    def columns(slot):
        rows = clusters_of(r_unit, slot)
        for j in range(GROUPS):
            row = jnp.broadcast_to(rows[j : j + 1, :], (LANES, LANES))
            r_col[slot, j * LANES : (j + 1) * LANES, :] = row.T

    columns(0)
    row_acc[...] = jnp.full_like(row_acc, -1.0)

    def landed(ref, sem):
        pltpu.make_async_copy(ref, ref, sem).wait()

    def r_wait(d, k):
        landed(r_unit.at[d, piece(k)], r_recv.at[d, k])

    def s_wait(s, k):
        landed(s_unit.at[s, up(k)], s_recv.at[s, k])

    def to_core_0(i, k):
        @pl.when(core == 1)
        def _():
            q1_copy(i, k).start()

    def hand_on(pieces):
        for k in pieces:
            s_wait(3, k)
            q1_copy(1, k).start()

    def score(r, s, s_clusters, peaks, best):
        scores = lax.dot_general(
            r_unit[r, HEAD:],
            s_unit[s, HEAD:],
            (((1,), (1,)), ((), ())),
            preferred_element_type=jnp.float32,
        )
        a_ids = r_col[r]
        for j in range(GROUPS):
            lanes = slice(j * LANES, (j + 1) * LANES)
            kept = jnp.where(a_ids == s_clusters[j : j + 1, :], scores[:, lanes], -1.0)
            best = jnp.maximum(best, kept)
            peaks[j] = jnp.maximum(peaks[j], jnp.max(kept.reshape(ROWS // 8, 8, LANES), axis=0))
        return best

    def rows_done(r, best):
        at = lax.rem(y + (0, 1, 3, 2)[r], 4)
        for j in range(GROUPS):
            part = best[j * LANES : (j + 1) * LANES, :].T
            row_all[n, at, j : j + 1, :] = jnp.max(part, axis=0, keepdims=True)

    def score_half(r, s, half, s_clusters, peaks, best):
        keys = pl.ds(pl.multiple_of(HEAD + half * (ROWS // 2), HEAD), ROWS // 2)
        scores = lax.dot_general(
            r_unit[r, HEAD:],
            s_unit[s, keys, :],
            (((1,), (1,)), ((), ())),
            preferred_element_type=jnp.float32,
        )
        a_ids = r_col[r]
        for j in range(GROUPS // 2):
            b_ids = jnp.where(half == 0, s_clusters[j : j + 1, :], s_clusters[j + 2 : j + 3, :])
            kept = jnp.where(a_ids == b_ids, scores[:, j * LANES : (j + 1) * LANES], -1.0)
            best = jnp.maximum(best, kept)
            peaks[j] = jnp.maximum(peaks[j], jnp.max(kept.reshape(ROWS // 8, 8, LANES), axis=0))
        return best

    def half_slot(s, half, done):
        s_clusters = clusters_of(s_unit, s)
        peaks = empty()[: GROUPS // 2]
        for r in range(4):
            done(r, score_half(r, s, half, s_clusters, peaks, row_acc[r]))
        for j in range(GROUPS // 2):
            col_acc[s, half * 2 + j] = peaks[j]

    def keep(r, best):
        row_acc[r] = best

    def score_near(s, peaks):
        s_clusters = clusters_of(s_unit, s)
        for r in range(3):
            row_acc[r] = score(r, s, s_clusters, peaks, row_acc[r])

    def empty():
        return [jnp.full((8, LANES), -1.0, jnp.float32)] * GROUPS

    def up_and_over(pieces):
        for k in pieces:
            s_wait(p_slot, k)
            f_copy(k).start()
            to_core_0(0, k)

    def tell(sem, where):
        pl.semaphore_signal(sem, inc=1, device_id=where, device_id_type=MESH)

    def say_ready():
        pl.semaphore_wait(seen, 1)
        tell(ready, device(plane + 1, n_p, core))

    def on_core(which, pieces, act):
        @pl.when(core == which)
        def _():
            for k in pieces:
                act(k)

    def relay(k):
        for slot, piece_of in ((2, k), (1, 2 + k)):
            r_wait(slot, piece_of)
            relay_copy(slot, piece_of).start()

    def late_q0():
        for i in (1, 0):
            q0_copy(i, LAST).start()
        q0_copy(0, 0).start()

    def r_wait_near():
        for k in range(2):
            r_wait(1, k)
            r_wait(2, 2 + k)
        columns(1)
        columns(2)

    def r_wait_far():
        for k in range(CHUNKS):
            r_wait(3, k)
        columns(3)

    def q0_wait(s):
        for k in (0, LAST):
            landed(s_unit.at[s, q0_rows(k)], s_recv.at[s, k])

    @pl.when(crosses_in)
    def _():
        relay(0)
        tell(seen, device(plane, n_x, core))
        on_core(0, (0,), lambda _: late_q0())
        relay(1)
        say_ready()

        @pl.loop(0, 6)
        def _(i):
            @pl.when(i == 0)
            def _():
                up_and_over((0, 1))
                r_wait_near()
                r_wait_far()
                on_core(1, (0, 1), q0_wait)

            @pl.when(i == 1)
            def _():
                up_and_over((2, 3))
                on_core(0, (0, 1), lambda k: s_wait(1, k))

            @pl.when(i == 2)
            def _():
                s_wait(f_slot, 0)
                to_core_0(1, 0)
                on_core(0, (LAST,), lambda k: s_wait(0, k))

            @pl.when(i == 3)
            def _():
                on_core(0, (2, 3, LAST), lambda k: s_wait(1, k))
                on_core(1, (LAST,), lambda k: s_wait(2, k))
                to_core_0(0, LAST)

            @pl.when(i == 4)
            def _():
                on_core(0, (1,), lambda k: s_wait(2, k))

            @pl.when(i == 5)
            def _():
                on_core(0, (0, 1), lambda k: s_wait(3, k))
                on_core(1, (0,), lambda _: hand_on((1, 2)))

            by_slot = jnp.logical_and(core == 1, i < 4)
            s = jnp.where(by_slot, i // 2, 2 * (i // 4) + lax.rem(i, 2))
            half = jnp.where(by_slot, lax.rem(i, 2), lax.rem(i, 4) // 2)
            half_slot(s, half, keep)

        on_core(1, (0,), lambda _: hand_on((3,)))
        on_core(1, (0,), lambda _: pl.semaphore_wait(ready, 1))
        on_core(1, (0,), lambda _: hand_on((LAST,)))
        for slot in (2, 3):
            on_core(0, (2, 3, LAST), lambda k, slot=slot: s_wait(slot, k))
        peaks = [empty()[: GROUPS // 2] for _ in range(2)]
        clusters_2, clusters_3 = clusters_of(s_unit, 2), clusters_of(s_unit, 3)
        for r in range(4):
            best = score_half(r, 2, 1, clusters_2, peaks[0], row_acc[r])
            rows_done(r, score_half(r, 3, 1, clusters_3, peaks[1], best))
        for i in range(2):
            for j in range(GROUPS // 2):
                col_acc[2 + i, 2 + j] = peaks[i][j]

    @pl.when(jnp.logical_not(crosses_in))
    def _():
        relay(0)
        tell(seen, device(plane, n_x, core))
        up_and_over((0,))
        on_core(0, (0,), lambda _: late_q0())
        relay(1)
        up_and_over((1,))
        up_and_over((2, 3))
        say_ready()
        s_wait(f_slot, 0)
        to_core_0(1, 0)
        s_wait(p_slot, LAST)
        to_core_0(0, LAST)
        r_wait_near()

        @pl.loop(0, 2)
        def _(s):
            @pl.when(jnp.logical_and(core == 0, s == 1))
            def _():
                for k in range(LAST + 1):
                    s_wait(1, k)

            @pl.when(core == 1)
            def _():
                q0_wait(s)

            peaks = empty()
            score_near(s, peaks)
            for j in range(GROUPS):
                col_acc[s, j] = peaks[j]

        @pl.when(core == 1)
        def _():
            hand_on((1, 2))

        r_wait_far()
        best = row_acc[3]
        for s in range(2):
            peaks = [col_acc[s, j] for j in range(GROUPS)]
            best = score(3, s, clusters_of(s_unit, s), peaks, best)
            for j in range(GROUPS):
                col_acc[s, j] = peaks[j]
        row_acc[3] = best

        @pl.when(core == 0)
        def _():
            for k in range(1, LAST + 1):
                s_wait(2, k)

        @pl.when(core == 1)
        def _():
            hand_on((3,))
            pl.semaphore_wait(ready, 1)
            hand_on((LAST,))

        peaks = empty()
        score_near(2, peaks)
        row_acc[3] = score(3, 2, clusters_of(s_unit, 2), peaks, row_acc[3])
        for j in range(GROUPS):
            col_acc[2, j] = peaks[j]

        @pl.when(core == 0)
        def _():
            for k in range(LAST + 1):
                s_wait(3, k)

        s_clusters = clusters_of(s_unit, 3)
        peaks = empty()
        for r in range(4):
            rows_done(r, score(r, 3, s_clusters, peaks, row_acc[r]))
        for j in range(GROUPS):
            col_acc[3, j] = peaks[j]

    def tail(src, dst, kind, where):
        return remote(src, dst, tail_send.at[kind], tail_recv.at[kind], where)

    def send_rows():
        for m in (
            *(device(plane, lax.rem(y + d, 4) * 2 + 1 - x, core) for d in (2, 1, 3)),
            *(y_peer(d) for d in (2, 1, 3)),
            device(plane, n_x, core),
        ):
            tail(row_all.at[n], row_all.at[n], 0, m).start()

    send_rows()

    for s in range(4):
        block = jnp.where(core == 0, s % 2, 1 - s // 2)
        x_0 = x_p if s < 2 else 1 - x_p
        x_1 = (x, 1 - x, x_p, 1 - x_p)[s]
        x_abs = jnp.where(core == 0, x_0, x_1)
        for j in range(GROUPS):
            peak = jnp.max(col_acc[s, j], axis=0, keepdims=True)
            col_src[block, x_abs, j : j + 1, :] = peak

    @pl.when(core == 0)
    def _():
        pl.semaphore_wait(ready, 1)

    for k in range(8):
        tail(col_src.at[0], col_all.at[0, n], 1, device(plane - 1, k, core)).start()
        tail(col_src.at[1], col_all.at[1, n], 1, device(plane - 1 + core, k, 1 - core)).start()


    for k in range(CHUNKS):
        y_copy(1, k).wait_send()
        y_copy(3, k).wait_send()
        relay_copy(1 if k >= 2 else 2, k).wait_send()
    for k in range(LAST + 1):
        p_copy(k).wait_send()
        f_copy(k).wait_send()
    for i in range(2):

        @pl.when(core == 0)
        def _():
            q0_copy(i, 0).wait_send()
            q0_copy(i, LAST).wait_send()

        @pl.when(core == 1)
        def _():
            for k in range(LAST + 1):
                q1_copy(i, k).wait_send()

    some = row_all.at[pl.ds(0, 7)]
    landed(some, tail_recv.at[0])
    landed(col_all, tail_recv.at[1])
    for y_abs in range(4):
        for x_abs in range(2):
            best = jnp.full((GROUPS, LANES), -1.0, jnp.float32)
            for y_from in range(4):
                best = jnp.maximum(best, row_all[y_from * 2 + x_abs, y_abs])
            for g in range(2):
                for x_from in range(2):
                    best = jnp.maximum(best, col_all[g, y_abs * 2 + x_from, x_abs])
            out[y_abs * 2 + x_abs] = best

    landed(some, tail_send.at[0])
    landed(col_all, tail_send.at[1])


def body(embeddings, projection, cluster_id):
    dma = pltpu.SemaphoreType.DMA
    operands = embeddings, projection, cluster_id.reshape(GROUPS, LANES)
    best = pl.pallas_call(
        kernel,
        out_shape=jax.ShapeDtypeStruct((8, GROUPS, LANES), jnp.float32),
        in_specs=[
            pl.BlockSpec(memory_space=pltpu.HBM),
            pl.BlockSpec(memory_space=pltpu.HBM),
            pl.BlockSpec(memory_space=pltpu.HBM),
        ],
        out_specs=pl.BlockSpec(memory_space=pltpu.VMEM),
        scratch_shapes=[
            pltpu.VMEM((ROWS, D), jnp.bfloat16),
            pltpu.VMEM((D, SK), jnp.bfloat16),
            pltpu.VMEM((GROUPS, LANES), jnp.int32),
            pltpu.VMEM((4, HEAD + ROWS, SK), jnp.bfloat16),
            pltpu.VMEM((4, HEAD + ROWS, SK), jnp.bfloat16),
            pltpu.VMEM((4, ROWS, LANES), jnp.float32),
            pltpu.VMEM((4, ROWS, LANES), jnp.float32),
            pltpu.VMEM((4, GROUPS, 8, LANES), jnp.float32),
            pltpu.VMEM((8, 4, GROUPS, LANES), jnp.float32),
            pltpu.VMEM((2, 2, GROUPS, LANES), jnp.float32),
            pltpu.VMEM((2, 8, 2, GROUPS, LANES), jnp.float32),
            dma((4,)),
            dma((2, CHUNKS)),
            dma((2, 2)),
            dma((4, CHUNKS)),
            dma((LAST + 1,)),
            dma((LAST + 1,)),
            dma((2, LAST + 1)),
            dma((4, LAST + 1)),
            dma((2,)),
            dma((2,)),
            pltpu.SemaphoreType.REGULAR,
            pltpu.SemaphoreType.REGULAR,
        ],
        compiler_params=pltpu.CompilerParams(
            collective_id=0, has_side_effects=True, vmem_limit_bytes=32 << 20
        ),
        name="best_match",
    )(*(pltpu.with_memory_space_constraint(a, pltpu.HBM) for a in operands))
    return best.reshape(8 * ROWS)


def solution(mesh):
    in_specs = (P(("wide", "narrow"), None), P(), P(("wide", "narrow")))
    out_specs = P("wide")
    return jax.shard_map(body, mesh=mesh, in_specs=in_specs, out_specs=out_specs, check_vma=False)
```

```python
import jax
import jax.numpy as jnp
from jax import lax
from jax.experimental import pallas as pl
from jax.experimental.pallas import tpu as pltpu
from jax.sharding import PartitionSpec as P

MESH = pl.DeviceIdType.MESH
ROWS = 512
SK = 256
D = 1024
CHUNKS = 4
CH = ROWS // CHUNKS
HEAD = 16
UP = ((0, 144), (144, 128), (272, 112), (384, 80), (464, 64))
LAST = len(UP) - 1
PLANES = 16
LANES = 128
GROUPS = ROWS // LANES


def device(plane, n, core):
    return (lax.rem(plane + PLANES, PLANES) * 2 + core, n)


def kernel(
    emb,
    proj,
    ids_in,
    out,
    emb_v,
    proj_v,
    ids,
    r_unit,
    s_unit,
    r_col,
    row_acc,
    col_acc,
    row_all,
    col_src,
    col_all,
    in_sem,
    y_send,
    relay_send,
    r_recv,
    p_send,
    f_send,
    q_send,
    s_recv,
    tail_send,
    tail_recv,
    ready,
    seen,
):
    wide, n = lax.axis_index("wide"), lax.axis_index("narrow")
    plane, core = wide // 2, lax.rem(wide, 2)
    y, x = n // 2, lax.rem(n, 2)
    n_x = y * 2 + 1 - x
    crosses_out = lax.rem(plane, 8) == 7
    crosses_in = lax.rem(plane, 8) == 0
    n_p = jnp.where(crosses_out, n_x, n)
    n_f = jnp.where(crosses_out, n, n_x)
    x_p = jnp.where(crosses_in, 1 - x, x)
    p_slot, f_slot = 2 * core, 2 + core

    first, rest = pl.ds(0, CH), pl.ds(CH, ROWS - CH)
    loads = [
        pltpu.make_async_copy(proj, proj_v, in_sem.at[0]),
        pltpu.make_async_copy(emb.at[first], emb_v.at[first], in_sem.at[1]),
        pltpu.make_async_copy(ids_in, ids, in_sem.at[2]),
        pltpu.make_async_copy(emb.at[rest], emb_v.at[rest], in_sem.at[3]),
    ]
    for copy in loads:
        copy.start()

    barrier = pltpu.get_barrier_semaphore()

    def greet(where):
        pl.semaphore_signal(barrier, inc=1, device_id=where, device_id_type=MESH)

    greet(device(plane - 1, n, core))
    greet(device(plane - 1, n_x, core))
    greet(device(plane, lax.rem(y + 1, 4) * 2 + x, core))
    greet(device(plane, lax.rem(y + 3, 4) * 2 + x, core))
    greet(device(plane, n_x, core))
    greet(device(plane, n, 1 - core))

    @pl.when(core == 1)
    def _():
        greet(device(plane, n_x, 0))

    def remote(src, dst, send, recv, where):
        return pltpu.make_async_remote_copy(
            src_ref=src,
            dst_ref=dst,
            send_sem=send,
            recv_sem=recv,
            device_id=where,
            device_id_type=MESH,
        )

    def piece(k):
        return pl.ds(HEAD + k * CH, CH) if k else pl.ds(0, HEAD + CH)

    def y_peer(d):
        return device(plane, lax.rem(y + d, 4) * 2 + x, core)

    def y_copy(d, k):
        slot = 2 if d == 1 else 1
        src, dst = r_unit.at[0, piece(k)], r_unit.at[slot, piece(k)]
        return remote(src, dst, y_send.at[slot - 1, k], r_recv.at[slot, k], y_peer(d))

    def relay_copy(slot, k):
        src, dst = r_unit.at[slot, piece(k)], r_unit.at[3, piece(k)]
        where = y_peer(3 if slot == 1 else 1)
        return remote(src, dst, relay_send.at[slot - 1, k % 2], r_recv.at[3, k], where)

    def up(k):
        return pl.ds(*UP[k])

    def p_copy(k):
        src, dst = r_unit.at[0, up(k)], s_unit.at[p_slot, up(k)]
        return remote(src, dst, p_send.at[k], s_recv.at[p_slot, k], device(plane + 1, n_p, core))

    def f_copy(k):
        here = s_unit.at[p_slot, up(k)] if k < LAST else r_unit.at[0, up(k)]
        where = device(plane, n_x, core) if k < LAST else device(plane + 1, n_f, core)
        return remote(here, s_unit.at[f_slot, up(k)], f_send.at[k], s_recv.at[f_slot, k], where)

    def q0_rows(k):
        return up(k) if k == LAST else pl.ds(0, UP[LAST][0])

    def q0_copy(i, k):
        src, dst = r_unit.at[0, q0_rows(k)], s_unit.at[i, q0_rows(k)]
        where = device(plane, n_x if i else n, 1)
        return remote(src, dst, q_send.at[i, k], s_recv.at[i, k], where)

    def q1_copy(i, k):
        src, dst = s_unit.at[2 + i, up(k)], s_unit.at[1 + 2 * i, up(k)]
        where = device(plane, n, 0)
        return remote(src, dst, q_send.at[i, k], s_recv.at[1 + 2 * i, k], where)

    loads[2].wait()
    clusters = jnp.concatenate(
        [ids[...].astype(jnp.float32), jnp.zeros((HEAD - GROUPS, LANES), jnp.float32)], axis=0
    )
    r_unit[0, :HEAD, :LANES] = clusters.astype(jnp.bfloat16)
    r_unit[0, :HEAD, LANES:] = jnp.zeros((HEAD, SK - LANES), jnp.bfloat16)

    def make_units(start, stop):
        sketch = jnp.dot(emb_v[start:stop, :], proj_v[...], preferred_element_type=jnp.float32)
        squares = jnp.sum(sketch * sketch, axis=1, keepdims=True)
        unit = (sketch * lax.rsqrt(squares + 1e-06)).astype(jnp.bfloat16)
        r_unit[0, HEAD + start : HEAD + stop, :] = unit

    loads[0].wait()
    loads[1].wait()
    make_units(0, CH)
    pl.semaphore_wait(barrier, 7 - core)
    p_copy(0).start()
    y_copy(1, 0).start()
    loads[3].wait()
    make_units(CH, ROWS)
    p_copy(1).start()
    p_copy(2).start()
    p_copy(3).start()
    p_copy(LAST).start()
    f_copy(LAST).start()
    y_copy(3, 2).start()
    y_copy(1, 1).start()
    y_copy(3, 3).start()
    y_copy(1, 2).start()
    y_copy(3, 0).start()
    y_copy(1, 3).start()
    y_copy(3, 1).start()

    @pl.when(core == 0)
    def _():
        q0_copy(1, 0).start()

    def clusters_of(unit, slot):
        return unit[slot, :HEAD, :LANES].astype(jnp.float32)

    def columns(slot):
        rows = clusters_of(r_unit, slot)
        for j in range(GROUPS):
            row = jnp.broadcast_to(rows[j : j + 1, :], (LANES, LANES))
            r_col[slot, j * LANES : (j + 1) * LANES, :] = row.T

    columns(0)
    row_acc[...] = jnp.full_like(row_acc, -1.0)

    def landed(ref, sem):
        pltpu.make_async_copy(ref, ref, sem).wait()

    def r_wait(d, k):
        landed(r_unit.at[d, piece(k)], r_recv.at[d, k])

    def s_wait(s, k):
        landed(s_unit.at[s, up(k)], s_recv.at[s, k])

    def to_core_0(i, k):
        @pl.when(core == 1)
        def _():
            q1_copy(i, k).start()

    def hand_on(pieces):
        for k in pieces:
            s_wait(3, k)
            q1_copy(1, k).start()

    def score(r, s, s_clusters, peaks, best):
        scores = lax.dot_general(
            r_unit[r, HEAD:],
            s_unit[s, HEAD:],
            (((1,), (1,)), ((), ())),
            preferred_element_type=jnp.float32,
        )
        a_ids = r_col[r]
        for j in range(GROUPS):
            lanes = slice(j * LANES, (j + 1) * LANES)
            kept = jnp.where(a_ids == s_clusters[j : j + 1, :], scores[:, lanes], -1.0)
            best = jnp.maximum(best, kept)
            peaks[j] = jnp.maximum(peaks[j], jnp.max(kept.reshape(ROWS // 8, 8, LANES), axis=0))
        return best

    def rows_done(r, best):
        at = lax.rem(y + (0, 1, 3, 2)[r], 4)
        for j in range(GROUPS):
            part = best[j * LANES : (j + 1) * LANES, :].T
            row_all[n, at, j : j + 1, :] = jnp.max(part, axis=0, keepdims=True)

    def score_half(r, s, half, s_clusters, peaks, best):
        keys = pl.ds(pl.multiple_of(HEAD + half * (ROWS // 2), HEAD), ROWS // 2)
        scores = lax.dot_general(
            r_unit[r, HEAD:],
            s_unit[s, keys, :],
            (((1,), (1,)), ((), ())),
            preferred_element_type=jnp.float32,
        )
        a_ids = r_col[r]
        for j in range(GROUPS // 2):
            b_ids = jnp.where(half == 0, s_clusters[j : j + 1, :], s_clusters[j + 2 : j + 3, :])
            kept = jnp.where(a_ids == b_ids, scores[:, j * LANES : (j + 1) * LANES], -1.0)
            best = jnp.maximum(best, kept)
            peaks[j] = jnp.maximum(peaks[j], jnp.max(kept.reshape(ROWS // 8, 8, LANES), axis=0))
        return best

    def half_slot(s, half, done):
        s_clusters = clusters_of(s_unit, s)
        peaks = empty()[: GROUPS // 2]
        for r in range(4):
            done(r, score_half(r, s, half, s_clusters, peaks, row_acc[r]))
        for j in range(GROUPS // 2):
            col_acc[s, half * 2 + j] = peaks[j]

    def keep(r, best):
        row_acc[r] = best

    def score_near(s, peaks):
        s_clusters = clusters_of(s_unit, s)
        for r in range(3):
            row_acc[r] = score(r, s, s_clusters, peaks, row_acc[r])

    def empty():
        return [jnp.full((8, LANES), -1.0, jnp.float32)] * GROUPS

    def up_and_over(pieces):
        for k in pieces:
            s_wait(p_slot, k)
            f_copy(k).start()
            to_core_0(0, k)

    def tell(sem, where):
        pl.semaphore_signal(sem, inc=1, device_id=where, device_id_type=MESH)

    def say_ready():
        pl.semaphore_wait(seen, 1)
        tell(ready, device(plane + 1, n_p, core))

    def on_core(which, pieces, act):
        @pl.when(core == which)
        def _():
            for k in pieces:
                act(k)

    def relay(k):
        for slot, piece_of in ((2, k), (1, 2 + k)):
            r_wait(slot, piece_of)
            relay_copy(slot, piece_of).start()

    def late_q0():
        for i in (1, 0):
            q0_copy(i, LAST).start()
        q0_copy(0, 0).start()

    def r_wait_near():
        for k in range(2):
            r_wait(1, k)
            r_wait(2, 2 + k)
        columns(1)
        columns(2)

    def r_wait_far():
        for k in range(CHUNKS):
            r_wait(3, k)
        columns(3)

    def q0_wait(s):
        for k in (0, LAST):
            landed(s_unit.at[s, q0_rows(k)], s_recv.at[s, k])

    @pl.when(crosses_in)
    def _():
        relay(0)
        tell(seen, device(plane, n_x, core))
        on_core(0, (0,), lambda _: late_q0())
        relay(1)
        say_ready()

        @pl.loop(0, 6)
        def _(i):
            @pl.when(i == 0)
            def _():
                up_and_over((0, 1))
                r_wait_near()
                r_wait_far()
                on_core(1, (0, 1), q0_wait)

            @pl.when(i == 1)
            def _():
                up_and_over((2, 3))
                on_core(0, (0, 1), lambda k: s_wait(1, k))

            @pl.when(i == 2)
            def _():
                s_wait(f_slot, 0)
                to_core_0(1, 0)
                on_core(0, (LAST,), lambda k: s_wait(0, k))

            @pl.when(i == 3)
            def _():
                on_core(0, (2, 3, LAST), lambda k: s_wait(1, k))
                on_core(1, (LAST,), lambda k: s_wait(2, k))
                to_core_0(0, LAST)

            @pl.when(i == 4)
            def _():
                on_core(0, (1,), lambda k: s_wait(2, k))

            @pl.when(i == 5)
            def _():
                on_core(0, (0, 1), lambda k: s_wait(3, k))
                on_core(1, (0,), lambda _: hand_on((1, 2)))

            by_slot = jnp.logical_and(core == 1, i < 4)
            s = jnp.where(by_slot, i // 2, 2 * (i // 4) + lax.rem(i, 2))
            half = jnp.where(by_slot, lax.rem(i, 2), lax.rem(i, 4) // 2)
            half_slot(s, half, keep)

        on_core(1, (0,), lambda _: hand_on((3,)))
        on_core(1, (0,), lambda _: pl.semaphore_wait(ready, 1))
        on_core(1, (0,), lambda _: hand_on((LAST,)))
        for slot in (2, 3):
            on_core(0, (2, 3, LAST), lambda k, slot=slot: s_wait(slot, k))
        peaks = [empty()[: GROUPS // 2] for _ in range(2)]
        clusters_2, clusters_3 = clusters_of(s_unit, 2), clusters_of(s_unit, 3)
        for r in range(4):
            best = score_half(r, 2, 1, clusters_2, peaks[0], row_acc[r])
            rows_done(r, score_half(r, 3, 1, clusters_3, peaks[1], best))
        for i in range(2):
            for j in range(GROUPS // 2):
                col_acc[2 + i, 2 + j] = peaks[i][j]

    @pl.when(jnp.logical_not(crosses_in))
    def _():
        relay(0)
        tell(seen, device(plane, n_x, core))
        up_and_over((0,))
        on_core(0, (0,), lambda _: late_q0())
        relay(1)
        up_and_over((1,))
        up_and_over((2, 3))
        say_ready()
        s_wait(f_slot, 0)
        to_core_0(1, 0)
        s_wait(p_slot, LAST)
        to_core_0(0, LAST)
        r_wait_near()

        @pl.loop(0, 2)
        def _(s):
            @pl.when(jnp.logical_and(core == 0, s == 1))
            def _():
                for k in range(LAST + 1):
                    s_wait(1, k)

            @pl.when(core == 1)
            def _():
                q0_wait(s)

            peaks = empty()
            score_near(s, peaks)
            for j in range(GROUPS):
                col_acc[s, j] = peaks[j]

        @pl.when(core == 1)
        def _():
            hand_on((1, 2))

        r_wait_far()
        best = row_acc[3]
        for s in range(2):
            peaks = [col_acc[s, j] for j in range(GROUPS)]
            best = score(3, s, clusters_of(s_unit, s), peaks, best)
            for j in range(GROUPS):
                col_acc[s, j] = peaks[j]
        row_acc[3] = best

        @pl.when(core == 0)
        def _():
            for k in range(1, LAST + 1):
                s_wait(2, k)

        @pl.when(core == 1)
        def _():
            hand_on((3,))
            pl.semaphore_wait(ready, 1)
            hand_on((LAST,))

        peaks = empty()
        score_near(2, peaks)
        row_acc[3] = score(3, 2, clusters_of(s_unit, 2), peaks, row_acc[3])
        for j in range(GROUPS):
            col_acc[2, j] = peaks[j]

        @pl.when(core == 0)
        def _():
            for k in range(LAST + 1):
                s_wait(3, k)

        s_clusters = clusters_of(s_unit, 3)
        peaks = empty()
        for r in range(4):
            rows_done(r, score(r, 3, s_clusters, peaks, row_acc[r]))
        for j in range(GROUPS):
            col_acc[3, j] = peaks[j]

    def tail(src, dst, kind, where):
        return remote(src, dst, tail_send.at[kind], tail_recv.at[kind], where)

    def send_rows():
        for m in (
            *(device(plane, lax.rem(y + d, 4) * 2 + 1 - x, core) for d in (2, 1, 3)),
            *(y_peer(d) for d in (2, 1, 3)),
            device(plane, n_x, core),
        ):
            tail(row_all.at[n], row_all.at[n], 0, m).start()

    send_rows()

    for s in range(4):
        block = jnp.where(core == 0, s % 2, 1 - s // 2)
        x_0 = x_p if s < 2 else 1 - x_p
        x_1 = (x, 1 - x, x_p, 1 - x_p)[s]
        x_abs = jnp.where(core == 0, x_0, x_1)
        for j in range(GROUPS):
            peak = jnp.max(col_acc[s, j], axis=0, keepdims=True)
            col_src[block, x_abs, j : j + 1, :] = peak

    @pl.when(core == 0)
    def _():
        pl.semaphore_wait(ready, 1)

    for k in range(8):
        tail(col_src.at[0], col_all.at[0, n], 1, device(plane - 1, k, core)).start()
        tail(col_src.at[1], col_all.at[1, n], 1, device(plane - 1 + core, k, 1 - core)).start()


    for k in range(CHUNKS):
        y_copy(1, k).wait_send()
        y_copy(3, k).wait_send()
        relay_copy(1 if k >= 2 else 2, k).wait_send()
    for k in range(LAST + 1):
        p_copy(k).wait_send()
        f_copy(k).wait_send()
    for i in range(2):

        @pl.when(core == 0)
        def _():
            q0_copy(i, 0).wait_send()
            q0_copy(i, LAST).wait_send()

        @pl.when(core == 1)
        def _():
            for k in range(LAST + 1):
                q1_copy(i, k).wait_send()

    some = row_all.at[pl.ds(0, 7)]
    landed(some, tail_recv.at[0])
    landed(col_all, tail_recv.at[1])
    for y_abs in range(4):
        for x_abs in range(2):
            best = jnp.full((GROUPS, LANES), -1.0, jnp.float32)
            for y_from in range(4):
                best = jnp.maximum(best, row_all[y_from * 2 + x_abs, y_abs])
            for g in range(2):
                for x_from in range(2):
                    best = jnp.maximum(best, col_all[g, y_abs * 2 + x_from, x_abs])
            out[y_abs * 2 + x_abs] = best

    landed(some, tail_send.at[0])
    landed(col_all, tail_send.at[1])


def body(embeddings, projection, cluster_id):
    dma = pltpu.SemaphoreType.DMA
    operands = embeddings, projection, cluster_id.reshape(GROUPS, LANES)
    best = pl.pallas_call(
        kernel,
        out_shape=jax.ShapeDtypeStruct((8, GROUPS, LANES), jnp.float32),
        in_specs=[
            pl.BlockSpec(memory_space=pltpu.HBM),
            pl.BlockSpec(memory_space=pltpu.HBM),
            pl.BlockSpec(memory_space=pltpu.HBM),
        ],
        out_specs=pl.BlockSpec(memory_space=pltpu.VMEM),
        scratch_shapes=[
            pltpu.VMEM((ROWS, D), jnp.bfloat16),
            pltpu.VMEM((D, SK), jnp.bfloat16),
            pltpu.VMEM((GROUPS, LANES), jnp.int32),
            pltpu.VMEM((4, HEAD + ROWS, SK), jnp.bfloat16),
            pltpu.VMEM((4, HEAD + ROWS, SK), jnp.bfloat16),
            pltpu.VMEM((4, ROWS, LANES), jnp.float32),
            pltpu.VMEM((4, ROWS, LANES), jnp.float32),
            pltpu.VMEM((4, GROUPS, 8, LANES), jnp.float32),
            pltpu.VMEM((8, 4, GROUPS, LANES), jnp.float32),
            pltpu.VMEM((2, 2, GROUPS, LANES), jnp.float32),
            pltpu.VMEM((2, 8, 2, GROUPS, LANES), jnp.float32),
            dma((4,)),
            dma((2, CHUNKS)),
            dma((2, 2)),
            dma((4, CHUNKS)),
            dma((LAST + 1,)),
            dma((LAST + 1,)),
            dma((2, LAST + 1)),
            dma((4, LAST + 1)),
            dma((2,)),
            dma((2,)),
            pltpu.SemaphoreType.REGULAR,
            pltpu.SemaphoreType.REGULAR,
        ],
        compiler_params=pltpu.CompilerParams(
            collective_id=0, has_side_effects=True, vmem_limit_bytes=32 << 20
        ),
        name="best_match",
    )(*(pltpu.with_memory_space_constraint(a, pltpu.HBM) for a in operands))
    return best.reshape(8 * ROWS)


def solution(mesh):
    in_specs = (P(("wide", "narrow"), None), P(), P(("wide", "narrow")))
    out_specs = P("wide")
    return jax.shard_map(body, mesh=mesh, in_specs=in_specs, out_specs=out_specs, check_vma=False)
```
